32 devices in a mesh: dp: 4 (over y, core), ffn: 8 (over z, x).
Axes of the slice: x: 2, y: 2, z: 4, core: 2. Of those that a mesh axis runs over, the one named last changes fastest.
Arguments:
- inputs: bfloat16 [32, 256, 1024], P(('dp', 'ffn')), may hold values from -6 to 6
- seg_ids: int32 [32, 256], P(('dp', 'ffn')), may hold values from 0 to 7, never falling along the last dimension, each value on 1 to 128 neighbouring positions
- w_query: bfloat16 [1024, 1024], replicated, may hold values from -0.1875 to 0.1875
- w_key: bfloat16 [1024, 1024], replicated, may hold values from -0.1875 to 0.1875
- w_value: bfloat16 [1024, 1024], replicated, may hold values from -0.1875 to 0.1875
- w_attn_out: bfloat16 [1024, 1024], replicated, may hold values from -1.5 to 1.5
- norm1_gain: float32 [1024], replicated, may hold values from 0.5 to 1.5
- norm1_bias: float32 [1024], replicated, may hold values from -1 to 1
- ffn_in: bfloat16 [4096, 1024], P('ffn'), may hold values from -0.1875 to 0.1875
- ffn_out: bfloat16 [4096, 1024], P('ffn'), may hold values from -0.09375 to 0.09375
- norm2_gain: float32 [1024], replicated, may hold values from 0.5 to 1.5
- norm2_bias: float32 [1024], replicated, may hold values from -1 to 1
- prefix_key: float32 [20, 1024], replicated, may hold values from -6 to 6
- prefix_value: float32 [20, 1024], replicated, may hold values from -6 to 6
- cotangent: bfloat16 [32, 256, 1024], P(('dp', 'ffn')), may hold values from -6 to 6
Outputs:
- layer_out: bfloat16 [32, 256, 1024], P(('dp', 'ffn'))
- input_grad: bfloat16 [32, 256, 1024], P(('dp', 'ffn'))
- prefix_key_grad: float32 [20, 1024], replicated
- prefix_value_grad: float32 [20, 1024], replicated
The draws below stay inside these ranges and needn't reach their ends.
Inputs may be any that keep to these rules, and one draw needn't show every extreme that they name: `seg_ids`: in each row the ids never fall and every id of 0 to 7 appears; id 7 marks the padding slots at the row's end; no id holds more than 128 slots of a row, and some id holds exactly 128.
All inputs are finite; a program needn't handle non-finite values.
Results may differ from the reference program's by a relative error of at most 0.017.
Values may be sent and summed in bfloat16 or wider, within the bound.
A program may use at most 192 MiB of HBM per device.

```python
import math
import jax
import jax.numpy as jnp
import numpy as np
from jax import lax

D = 1024
HEADS = 16
FF = 4096
HEAD_DIM = 64
PREF = 20
PAIRS = 7
SEG_MOST = 128
SLOTS = 256
ROWS = 32


def levels(stream_key, extent, cuts, least, high):
    factor_of = 1.0
    for dim, parts in cuts:
        heights = jax.random.uniform(jax.random.fold_in(jax.random.fold_in(stream_key, 6), dim), (parts,), jnp.float32, least / len(cuts), high / len(cuts))
        factor_of = factor_of * jnp.repeat(jnp.exp(heights), extent[dim] // parts).reshape((-1,) + (1,) * (len(extent) - 1 - dim))
    return factor_of


def profile(amount, total, bound, skew):
    loads = [(1 << 20) // math.isqrt(rank ** skew) + 1 for rank in range(2, amount + 1)]
    rest, counts = total - bound - (amount - 1), [1] * (amount - 1)
    while rest > 0:
        candidates = [i for i in range(amount - 1) if counts[i] < bound]
        mass, left = sum([loads[i] for i in candidates]), rest
        for i in candidates:
            addition = min(bound - counts[i], max(1, left * loads[i] // mass), rest)
            counts[i] = counts[i] + addition
            rest = rest - addition
    return np.array([bound] + counts)


def uneven_parts(rng, number_of, total, reach, skew):
    if number_of == 2:
        one = jax.random.randint(rng, (), max(1, total - reach), min(reach, total - 1) + 1)
        return jnp.stack([one, total - one])
    tallies = jnp.asarray(profile(number_of, total, reach, skew), jnp.int32)
    couples = (number_of - 1) // 2
    giver, sink = tallies[1:1 + 2 * couples:2], tallies[2:2 + 2 * couples:2]
    margin = jnp.minimum(giver - 1, reach - sink)
    passed = jax.random.randint(jax.random.fold_in(rng, 1), (couples,), 0, 1 << 20) % (margin + 1)
    tallies = tallies.at[1:1 + 2 * couples:2].set(giver - passed).at[2:2 + 2 * couples:2].set(sink + passed)
    return tallies[jax.random.permutation(jax.random.fold_in(rng, 2), number_of)]


def scatter_about(own_key, shape, scale, most, cuts=(), kind=jnp.bfloat16):
    level = levels(own_key, shape, cuts, -0.22, 0.18) if cuts else 1.0
    values = jax.random.normal(own_key, shape, jnp.float32) * scale * level
    return jnp.minimum(jnp.maximum(values, -most), most).astype(kind)


def setup_inputs(seed: int = 0) -> dict:
    seeds = jax.random.split(jax.random.key(seed), 16)
    return {
        "inputs": scatter_about(seeds[0], (ROWS, SLOTS, D), 1.0, 6.0, ((0, 32),)),
        "seg_ids": jax.vmap(lambda own: jnp.searchsorted(jnp.cumsum(uneven_parts(own, PAIRS + 1, SLOTS, SEG_MOST, 0)), jnp.arange(SLOTS), side="right"))(jax.random.split(seeds[1], ROWS)).reshape((ROWS, SLOTS)).astype(jnp.int32),
        "w_query": scatter_about(seeds[2], (D, D), D ** -0.5, 0.1875),
        "w_key": scatter_about(seeds[3], (D, D), D ** -0.5, 0.1875),
        "w_value": scatter_about(seeds[4], (D, D), D ** -0.5, 0.1875),
        "w_attn_out": scatter_about(seeds[5], (D, D), (D // 64) ** -0.5, 1.5),
        "norm1_gain": jnp.clip(1.0 + 0.1 * jax.random.normal(seeds[6], (D,), jnp.float32), 0.5, 1.5),
        "norm1_bias": scatter_about(seeds[7], (D,), 0.2, 1.0, (), jnp.float32),
        "ffn_in": scatter_about(seeds[8], (FF, D), D ** -0.5, 0.1875, ((0, 8),)),
        "ffn_out": scatter_about(seeds[9], (FF, D), FF ** -0.5, 0.09375, ((0, 8),)),
        "norm2_gain": jnp.clip(1.0 + 0.1 * jax.random.normal(seeds[10], (D,), jnp.float32), 0.5, 1.5),
        "norm2_bias": scatter_about(seeds[11], (D,), 0.2, 1.0, (), jnp.float32),
        "prefix_key": scatter_about(seeds[12], (PREF, D), 1.0, 6.0, (), jnp.float32),
        "prefix_value": scatter_about(seeds[13], (PREF, D), 1.0, 6.0, (), jnp.float32),
        "cotangent": scatter_about(seeds[14], (ROWS, SLOTS, D), 1.0, 6.0, ((0, 32),)),
    }


@jax.custom_vjp
def low(v):
    return lax.optimization_barrier(v.astype(jnp.bfloat16)).astype(jnp.float32)

@jax.custom_vjp
def low_back(v):
    return v

def low_keep(v):
    return (low(v), None)

def low_pass(kept, grad):
    return (grad,)

def back_keep(v):
    return (v, None)

def back_low(kept, grad):
    return (low(grad),)
low.defvjp(low_keep, low_pass)
low_back.defvjp(back_keep, back_low)
HIGH = lax.Precision.HIGHEST
EPS = 1e-05
NEG = -1e+30

def layer_norm(resid, gain, bias):
    center = resid - lax.optimization_barrier(jnp.mean(resid, axis=-1, keepdims=True))
    spread = lax.optimization_barrier(jnp.mean(center * center, axis=-1, keepdims=True))
    return center * lax.rsqrt(spread + EPS) * gain + bias

def forward(inputs, prefix_key, prefix_value, weights, seg_block):
    w_query, w_key, w_value, w_attn_out, norm1_gain, norm1_bias, ffn_in, ffn_out, norm2_gain, norm2_bias = weights
    count = inputs.shape[0]
    scale = HEAD_DIM ** (-0.5)

    def split_heads(t):
        return t.reshape(count, SLOTS, HEADS, HEAD_DIM)
    query = split_heads(low(low_back(jnp.einsum('rsd,de->rse', inputs, w_query, precision=HIGH) * scale)))
    key = split_heads(low(low_back(jnp.einsum('rsd,de->rse', inputs, w_key, precision=HIGH))))
    value = split_heads(low(low_back(jnp.einsum('rsd,de->rse', inputs, w_value, precision=HIGH))))
    pkey = low(prefix_key).reshape(PREF, HEADS, HEAD_DIM)
    pval = low(prefix_value).reshape(PREF, HEADS, HEAD_DIM)
    pref_scores = jnp.einsum('rqhd,phd->rhqp', query, pkey, precision=HIGH)
    cont_scores = jnp.einsum('rqhd,rkhd->rhqk', query, key, precision=HIGH)
    scores = low_back(jnp.concatenate([pref_scores, cont_scores], axis=-1))
    live = seg_block < PAIRS
    same = (seg_block[:, :, None] == seg_block[:, None, :]) & live[:, None, :]
    visible = jnp.concatenate([jnp.ones((count, SLOTS, PREF), dtype=bool), same], axis=-1)[:, None]
    scores = jnp.where(visible, scores, NEG)
    top = lax.optimization_barrier(jnp.max(scores, axis=-1, keepdims=True))
    expo = jnp.exp(scores - top)
    probs = low(expo / lax.optimization_barrier(jnp.sum(expo, axis=-1, keepdims=True)))
    mixed = jnp.einsum('rhqp,phd->rqhd', probs[..., :PREF], pval, precision=HIGH)
    mixed = mixed + jnp.einsum('rhqk,rkhd->rqhd', probs[..., PREF:], value, precision=HIGH)
    mixed = low(low_back(mixed.reshape(count, SLOTS, D)))
    attn = low_back(jnp.einsum('rsd,de->rse', mixed, w_attn_out, precision=HIGH))
    hidden = layer_norm(inputs + attn, norm1_gain, norm1_bias)
    pre = low_back(jnp.einsum('rsd,fd->rsf', low(hidden), ffn_in, precision=HIGH))
    act = low(jax.nn.gelu(pre, approximate=False))
    ffn = low_back(jnp.einsum('rsf,fd->rsd', act, ffn_out, precision=HIGH))
    return layer_norm(hidden + ffn, norm2_gain, norm2_bias)

def reference(inputs, seg_ids, w_query, w_key, w_value, w_attn_out, norm1_gain, norm1_bias, ffn_in, ffn_out, norm2_gain, norm2_bias, prefix_key, prefix_value, cotangent):
    weights = tuple((w.astype(jnp.float32) for w in (w_query, w_key, w_value, w_attn_out, norm1_gain, norm1_bias, ffn_in, ffn_out, norm2_gain, norm2_bias)))
    live = (seg_ids < PAIRS).astype(jnp.float32)
    block = math.gcd(ROWS, max(1, 4096 // SLOTS))
    steps = ROWS // block

    def shaped(t):
        return t.reshape((steps, block) + t.shape[1:])

    def step(carry, pieces):
        x_block, seg_block, cot_block, live_block = pieces

        def local(x_in, pk, pv):
            return forward(x_in, pk, pv, weights, seg_block)
        result, pull = jax.vjp(local, x_block.astype(jnp.float32), prefix_key.astype(jnp.float32), prefix_value.astype(jnp.float32))
        grad_x, grad_pk, grad_pv = pull(cot_block.astype(jnp.float32) * live_block[..., None])
        return ((carry[0] + grad_pk, carry[1] + grad_pv), (result.astype(jnp.bfloat16), grad_x.astype(jnp.bfloat16)))
    zeros = jnp.zeros((PREF, D), jnp.float32)
    (grad_pk, grad_pv), (outs, grads) = lax.scan(step, (zeros, zeros), (shaped(inputs), shaped(seg_ids), shaped(cotangent), shaped(live)))
    return (outs.reshape(ROWS, SLOTS, D), grads.reshape(ROWS, SLOTS, D), grad_pk, grad_pv)
```

```python
import functools

import jax
import jax.numpy as jnp
from jax import lax
from jax.experimental import pallas as pl
from jax.experimental.pallas import tpu as pltpu
from jax.sharding import PartitionSpec as P

HEADS = 16
PREF = 20
PAIRS = 7
EPS = 1e-05
NEG = -1e30
QUAD = 4
LANES = 256
PAD = 32
HELD = 24
ROWB = 32
F32 = jnp.float32
BF16 = jnp.bfloat16


def nt(a, b):
    return lax.dot_general(a, b, (((1,), (1,)), ((), ())), preferred_element_type=F32)


def nn(a, b):
    return lax.dot_general(a, b, (((1,), (0,)), ((), ())), preferred_element_type=F32)


def head_mask(shape, h):
    return lax.broadcasted_iota(jnp.int32, shape, 1) // 64 == h


def normalize(r):
    center = r - jnp.mean(r, axis=-1, keepdims=True)
    spread = jnp.mean(center * center, axis=-1, keepdims=True)
    rstd = lax.rsqrt(spread + EPS)
    return center * rstd, rstd


def norm_back(dn, n, rstd):
    return rstd * (dn - jnp.mean(dn, axis=-1, keepdims=True) - n * jnp.mean(dn * n, axis=-1, keepdims=True))


def split_dot(a, ones):
    hi = a.astype(BF16)
    return nn(hi, ones) + nn((a - hi.astype(F32)).astype(BF16), ones)


def gelu_parts(pre):
    cdf = 0.5 * (1.0 + lax.erf(pre * 0.7071067811865476))
    return pre * cdf, cdf + pre * (0.3989422804014327 * jnp.exp(-0.5 * pre * pre))


MESH_ID = pl.DeviceIdType.MESH
DEPTH = 4
SENDS = 200
PART_ROWS = (64, 64, 80, 80, 80, 80, 64)
PART_OFF = (0, 64, 128, 208, 288, 368, 448)
MAIN = 448
FAR = 64
A0, A1, B0, B1, C0, C1, DD = range(7)


class Gather:
    def __init__(self, w, shards, ssem, rsem, bsem):
        self.w, self.shards, self.ssem, self.rsem, self.bsem = w, shards, ssem, rsem, bsem
        d, f = lax.axis_index("dp"), lax.axis_index("ffn")
        self.y, self.c = d // 2, lax.rem(d, 2)
        self.z, self.x = f // 2, lax.rem(f, 2)
        self.sent = []
        self.dev = {
            "core": (self.y * 2 + 1 - self.c, f),
            "y": ((1 - self.y) * 2 + self.c, f),
            "x": (d, self.z * 2 + 1 - self.x),
            1: (d, jnp.minimum(self.z + 1, DEPTH - 1) * 2 + self.x),
            -1: (d, jnp.maximum(self.z - 1, 0) * 2 + self.x),
        }
        self.can = {1: lambda: self.z < DEPTH - 1, -1: lambda: self.z > 0, "x": None, "y": None, "core": None}

    def part(self, name):
        if name[0] in "PO":
            plane = self.y if name[0] == "P" else 1 - self.y
            i = int(name[1])
            return pl.multiple_of(PART_OFF[B0 + i] + plane * 160, 16), 80, B0 + i + 2 * plane
        i = {"A0": A0, "A1": A1, "D": DD}[name]
        return PART_OFF[i], PART_ROWS[i], i

    def place(self, m, s, off, rows, num):
        if isinstance(num, int) and num == DD:
            start = self.shards * MAIN + s * FAR
        else:
            start = s * MAIN + off
        return self.w.at[m, pl.ds(pl.multiple_of(start, 16), rows)]

    def copy(self, to, s, part, slot, m=None):
        off, rows, num = part
        ref = self.place(self.c if m is None else m, s, off, rows, num)
        sems = self.bsem if to == "core" else self.rsem
        return pltpu.make_async_remote_copy(
            src_ref=ref, dst_ref=ref, send_sem=self.ssem.at[slot], recv_sem=sems.at[s, num], device_id=self.dev[to],
            device_id_type=MESH_ID,
        )

    def send(self, to, s, name):
        part = self.part(name)
        desc = self.copy(to, s, part, len(self.sent))
        can = self.can[to]
        self.sent.append((self.conds + (() if can is None else (can,)), part[1]))
        if can is None:
            desc.start()
        else:
            pl.when(can())(desc.start)

    conds = ()

    def when(self, cond, fn):
        if cond is None:
            fn()
            return
        self.conds = self.conds + (cond,)
        pl.when(cond())(fn)
        self.conds = self.conds[:-1]

    def shard(self, dz, column):
        return jnp.clip(self.z + dz, 0, DEPTH - 1) * 2 + (self.x if column == 0 else 1 - self.x)

    def wait(self, s, name):
        self.copy("x", s, self.part(name), 0).wait_recv()

    def step(self, k):
        if k == 0:
            return [(0, None, 0)]
        if k == 1:
            return [(1, self.can[1], 1), (-1, self.can[-1], -1)]
        dz = jnp.where(self.z < DEPTH // 2, k, -k)
        if k == 2:
            return [(dz, None, None)]
        return [(dz, lambda: jnp.logical_or(self.z == 0, self.z == DEPTH - 1), None)]

    def along(self, dz, sign, s, name):
        if sign is None:
            back = jnp.where(self.z < DEPTH // 2, -1, 1)
            self.dev["back"] = (lax.axis_index("dp"), jnp.clip(self.z + back, 0, DEPTH - 1) * 2 + self.x)
            self.can["back"] = lambda: jnp.logical_or(self.z == 1, self.z == DEPTH - 2)
            self.send("back", s, name)
        elif sign:
            self.send(-sign, s, name)

    def from_z(self, k, name):
        for dz, cond, sign in self.step(k):
            def go(dz=dz, sign=sign):
                s = self.shard(dz, 0)
                self.wait(s, name)
                if k < 3:
                    self.along(dz, sign, s, name)
                if name[0] == "P":
                    self.send("y", s, name)
                self.send("x", s, name)
                self.send("core", s, name)
            self.when(cond, go)

    def from_x(self, k, name):
        for dz, cond, sign in self.step(k):
            def go(dz=dz):
                s = self.shard(dz, 1)
                self.wait(s, name)
                if name[0] == "P":
                    self.send("y", s, name)
                if name == "D":
                    self.send(1, s, name)
                    self.send(-1, s, name)
                self.send("core", s, name)
            self.when(cond, go)

    def far(self, k, column):
        for dz, cond, sign in self.step(k):
            def go(dz=dz, sign=sign):
                s = self.shard(dz, column)
                self.wait(s, "D")
                if k < 3:
                    self.along(dz, sign, s, "D")
                self.send("core", s, "D")
            self.when(cond, go)

    def from_y(self, k, column, name):
        for dz, cond, sign in self.step(k):
            def go(dz=dz):
                s = self.shard(dz, column)
                self.wait(s, name)
                self.send("core", s, name)
            self.when(cond, go)

    def sibling(self, k, column, names):
        for dz, cond, sign in self.step(k):
            def go(dz=dz):
                s = self.shard(dz, column)
                for name in names:
                    self.copy("core", s, self.part(name), 0, 1 - self.c).wait_recv()
            self.when(cond, go)

    def meet(self):
        bar = pltpu.get_barrier_semaphore()
        y, z, x, c = self.y, self.z, self.x, self.c
        others = [(y * 2 + 1 - c, z * 2 + x)]
        others += [(yy * 2 + c, z * 2 + xx) for yy, xx in ((y, 1 - x), (1 - y, x), (1 - y, 1 - x))]
        others += [(y * 2 + c, lax.rem(z + i, DEPTH) * 2 + x) for i in range(1, DEPTH)]
        for dev in others:
            pl.semaphore_signal(bar, inc=1, device_id=dev, device_id_type=MESH_ID)
        pl.semaphore_wait(bar, len(others))

    def finish(self):
        for slot, (conds, rows) in enumerate(self.sent):
            ref = self.w.at[0, pl.ds(0, rows)]
            desc = pltpu.make_async_remote_copy(
                src_ref=ref, dst_ref=ref, send_sem=self.ssem.at[slot], recv_sem=self.rsem.at[0, 0], device_id=self.dev["x"],
                device_id_type=MESH_ID,
            )
            if conds:
                pl.when(functools.reduce(jnp.logical_and, [c() for c in conds]))(desc.wait_send)
            else:
                desc.wait_send()

    def local(self, fin, fout, sem):
        s = self.shard(0, 0)
        out = []
        for m, src in enumerate((fin, fout)):
            out.append(pltpu.make_async_copy(src.at[pl.ds(0, MAIN)], self.place(m, s, 0, MAIN, 0), sem.at[2 * m]))
            out.append(pltpu.make_async_copy(src.at[pl.ds(MAIN, FAR)], self.place(m, s, MAIN, FAR, DD), sem.at[2 * m + 1]))
        for c in out:
            c.start()
        return out


def run_events(g, toks):
    for ev in toks:
        kind, k, name = ev[0], ev[1], ev[2:]
        if kind == "s":
            for to in ("x",) if k == "x" else (1, -1):
                g.send(to, g.shard(0, 0), ev[3:])
        elif kind == "z":
            g.from_z(int(k), name)
        elif kind == "x":
            g.from_x(int(k), name)
        elif kind in "de":
            g.far(int(k), int(kind == "e"))
        elif kind in "Yy":
            g.from_y(int(k), int(kind == "y"), name)


ORDER = (
    "sx:P1", "sz:P1", "sx:A0", "sz:P0", "x0P1", "sx:P0", "sx:A1", "z1P1", "sx:D", "CM", "z1P0", "sz:D", "x0P0", "CQ0", "x0A1", "sz:A1", "z2P0", "sz:A0", "y0O1",
    "z2P1", "CQ1", "x0D", "CQ2", "CQ3", "x1P1", "z3P0", "z1A1", "z3P1", "z1A0", "x0A0", "CA0", "e1", "Y1O0", "x3P0", "z2A1", "y0O0", "x1P0", "CA1", "CA2", "Y3O0", "Y2O1",
    "CA3", "CL", "y3O0", "d1", "x2P1", "x2P0", "z2A0", "Y1O1", "F0", "y1O1", "x1A1", "y1O0", "x1A0", "z3A1", "Y2O0", "e2", "d2", "x3P1", "F1", "x2A0", "Y3O1", "y2O1",
    "x2A1", "z3A0", "y2O0", "x3A1", "F2", "x3A0", "y3O1", "d3", "e3", "F3", "G",
)


class Reduce:
    def __init__(self, g, part, sib, got, along, total, ssem, rsem):
        self.g, self.part, self.sib, self.got, self.along, self.total = g, part, sib, got, along, total
        self.ssem, self.rsem = ssem, rsem
        self.sent = []
        y, x, z, c = g.y, g.x, g.z, g.c
        d, f = lax.axis_index("dp"), lax.axis_index("ffn")
        self.mine = y * 2 + x
        self.mates = [((y if a == 0 else 1 - y), (x if b == 0 else 1 - x)) for a, b in ((0, 1), (1, 0), (1, 1))]
        self.mate_dev = [(yy * 2 + c, z * 2 + xx) for yy, xx in self.mates]
        self.far_z = [lax.rem(z + i, DEPTH) for i in range(1, DEPTH)]

    def push(self, src, dst, recv, dev):
        desc = pltpu.make_async_remote_copy(
            src_ref=src, dst_ref=dst, send_sem=self.ssem.at[len(self.sent)], recv_sem=self.rsem.at[recv], device_id=dev,
            device_id_type=MESH_ID,
        )
        desc.start()
        self.sent.append(desc)

    def pull(self, dst, recv):
        pltpu.make_async_remote_copy(
            src_ref=dst, dst_ref=dst, send_sem=self.ssem.at[0], recv_sem=self.rsem.at[recv], device_id=self.g.dev["core"],
            device_id_type=MESH_ID,
        ).wait_recv()

    def piece(self, i):
        return pl.ds(pl.multiple_of(i * LANES, LANES), LANES)

    def step0(self):
        self.push(self.part.at[1 - self.g.c], self.sib, 0, self.g.dev["core"])

    def step1(self):
        self.pull(self.sib, 0)
        self.sib[...] = self.sib[...] + self.part[self.g.c]
        for i, (yy, xx) in enumerate(self.mates):
            self.push(self.sib.at[:, self.piece(yy * 2 + xx)], self.got.at[i], 1 + i, self.mate_dev[i])

    def step2(self):
        for i in range(3):
            self.pull(self.got.at[i], 1 + i)
        z = self.g.z
        self.along[z] = (self.sib[:, self.piece(self.mine)] + self.got[0]) + (self.got[1] + self.got[2])
        for zz in self.far_z:
            self.push(self.along.at[z], self.along.at[z], 4 + z, (lax.axis_index("dp"), zz * 2 + self.g.x))

    def step3(self):
        for zz in self.far_z:
            self.pull(self.along.at[zz], 4 + zz)
        cols = self.piece(self.mine)
        c = self.g.c
        self.total[c, :, cols] = (self.along[0] + self.along[1]) + (self.along[2] + self.along[3])
        mine = self.total.at[c, :, cols]
        for dev in self.mate_dev:
            self.push(mine, mine, 8 + self.mine, dev)
        self.push(mine, mine, 12 + self.mine, self.g.dev["core"])

    def step4(self):
        c = self.g.c
        for yy, xx in self.mates:
            i = yy * 2 + xx
            ref = self.total.at[c, :, self.piece(i)]
            self.pull(ref, 8 + i)
            self.push(ref, ref, 12 + i, self.g.dev["core"])
        for i in range(4):
            self.pull(self.total.at[1 - c, :, self.piece(i)], 12 + i)
        for desc in self.sent:
            desc.wait_send()


def kernel(
    remote,
    x_hbm, seg_ref, wq_hbm, wk_hbm, wv_hbm, wo_hbm, g1, b1, fin_hbm, fout_hbm, g2, b2, pk_ref, pv_ref, cot_hbm,
    out_hbm, gin_hbm, dpk_ref, dpv_ref,
    x, cot, wq, wk, wv, wo, w, q, k, v, km, qm, vm, prob, prob_t, ppref, mixed, mixed_low, n1, rstd1, hidden, hid_low,
    dgelu, gp, acc, gr2, glow, bias, live, pad_k, pad_v, ds, ds_t, outv, dq, dk, dv, sem_in, sem_w, sem_out,
    part, *comm,
):
    slots, width = x.shape
    units = w.shape[1]
    nq = width // LANES
    srcs = [(x_hbm, x), (wq_hbm, wq), (wk_hbm, wk), (wv_hbm, wv), (wo_hbm, wo), (cot_hbm, cot)]
    loads = [pltpu.make_async_copy(s, d, sem_in.at[i]) for i, (s, d) in enumerate(srcs)]
    if remote:
        ssem, rsem, bsem, sib, got, along, total, red_s, red_r = comm
        g = Gather(w, units // (MAIN + FAR), ssem, rsem, bsem)
        red = Reduce(g, part, sib, got, along, total, red_s, red_r)
        wloads = g.local(fin_hbm, fout_hbm, sem_w)
    else:
        wloads = [pltpu.make_async_copy(src, w.at[m], sem_w.at[m]) for m, src in enumerate((fin_hbm, fout_hbm))]
    for c in loads[:4]:
        c.start()
    if not remote:
        for c in wloads:
            c.start()
    for c in loads[4:]:
        c.start()
    bd_shape = (QUAD * PAD, LANES)
    block_diag = lax.broadcasted_iota(jnp.int32, bd_shape, 0) // PAD == lax.broadcasted_iota(jnp.int32, bd_shape, 1) // 64
    lane = lax.broadcasted_iota(jnp.int32, (1, QUAD * PAD), 1)

    def cols_of(j):
        return slice(j * LANES, (j + 1) * LANES)

    def pref_bias(h):
        return jnp.where((lane // PAD == h) & (lane % PAD < PREF), 0.0, NEG)

    def block(ref, j):
        part = ref[:, cols_of(j)]
        return jnp.where(block_diag, jnp.concatenate([part] * QUAD, axis=0), 0.0).astype(BF16)

    def masks():
        seg_row = jnp.broadcast_to(seg_ref[...].astype(F32), (slots, slots))
        seg_col = seg_row.T
        bias[...] = jnp.where((seg_row == seg_col) & (seg_row < PAIRS), 0.0, NEG)
        live[...] = (seg_col[:, :128] < PAIRS).astype(F32)
        pad_k[...] = jnp.zeros_like(pad_k)
        pad_v[...] = jnp.zeros_like(pad_v)
        pad_k[0:PREF, :] = pk_ref[...]
        pad_v[0:PREF, :] = pv_ref[...]

    def project(j):
        cols = cols_of(j)
        if j == 0:
            for i in range(4):
                loads[i].wait()
        q[:, cols] = (nn(x[...], wq[:, cols]) * 0.125).astype(BF16)
        k[:, cols] = nn(x[...], wk[:, cols]).astype(BF16)
        v[:, cols] = nn(x[...], wv[:, cols]).astype(BF16)
        for h in range(QUAD):
            rows = slice(h * slots, (h + 1) * slots)
            keep = head_mask((slots, LANES), h)
            qm[j, rows, :] = jnp.where(keep, q[:, cols], jnp.zeros((), BF16))
            km[j, rows, :] = jnp.where(keep, k[:, cols], jnp.zeros((), BF16))
            vm[j, rows, :] = jnp.where(keep, v[:, cols], jnp.zeros((), BF16))
        km[j, QUAD * slots:, :] = block(pad_k, j)
        vm[j, QUAD * slots:, :] = block(pad_v, j)

    def attend(j):
        cols = cols_of(j)
        sp_all = nt(q[:, cols], km[j, QUAD * slots:, :])
        pp_all = jnp.zeros((slots, QUAD * PAD), F32)
        for h in range(QUAD):
            rows = slice(h * slots, (h + 1) * slots)
            s = nt(q[:, cols], km[j, rows, :]) + bias[...]
            sp = sp_all + pref_bias(h)
            top = jnp.maximum(jnp.max(s, axis=-1, keepdims=True), jnp.max(sp, axis=-1, keepdims=True))
            e = jnp.exp(s - top)
            ep = jnp.exp(sp - top)
            inv = 1.0 / (jnp.sum(e, axis=-1, keepdims=True) + jnp.sum(ep, axis=-1, keepdims=True))
            p = e * inv
            prob[j * QUAD + h] = p
            ds[:, rows] = p.astype(BF16)
            prob_t[j, :, rows] = p.T.astype(BF16)
            pp_all = pp_all + ep * inv
        ppref[j] = pp_all
        ds[:, QUAD * slots:] = pp_all.astype(BF16)
        o = nn(ds[...], vm[j])
        mixed[:, cols] = o
        mixed_low[:, cols] = o.astype(BF16)

    def norm1():
        loads[4].wait()
        for j in range(nq):
            acc[:, cols_of(j)] = nn(mixed_low[...], wo[:, cols_of(j)])

        def rows_of(i, carry):
            r = pl.ds(pl.multiple_of(i * ROWB, ROWB), ROWB)
            n, rstd = normalize(x[r, :].astype(F32) + acc[r, :])
            n1[r, :] = n
            rstd1[r, :] = jnp.broadcast_to(rstd, (ROWB, 128))
            h = n * g1[...] + b1[...]
            hidden[r, :] = h
            hid_low[r, :] = h.astype(BF16)
            acc[r, :] = jnp.zeros((ROWB, width), F32)
            return carry

        lax.fori_loop(0, slots // ROWB, rows_of, 0)

    def feed(base, sizes):
        at, total = 0, sum(sizes)
        for n in sizes:
            act, slope = gelu_parts(nt(hid_low[...], w[0, pl.ds(base + at, n), :]))
            dgelu[:, pl.ds(base + at, n)] = slope
            gp[:, at:at + n] = act.astype(BF16)
            at += n
        for j in range(nq):
            acc[:, cols_of(j)] += nn(gp[:, :total], w[1, pl.ds(base, total), cols_of(j)])

    if remote:
        g.meet()
        for c in wloads:
            c.wait()
        pair = 2 * MAIN
        names = ("A0", "A1", "P0", "P1", "O0", "O1")
        for tok in ORDER:
            kind = tok[0]
            if kind == "C":
                step = tok[1:]
                if step == "M":
                    masks()
                elif step == "L":
                    norm1()
                elif step[0] == "Q":
                    project(int(step[1]))
                else:
                    attend(int(step[1]))
            elif kind == "F":
                dist = int(tok[1])
                if dist:
                    g.sibling(dist, 0, names)
                g.sibling(dist, 1, names)
                for dz, cond, sign in g.step(dist):
                    def go(dz=dz):
                        where = jnp.clip(g.z + dz, 0, DEPTH - 1)
                        feed(pl.multiple_of(where * pair, 128), (256, 256, 256, 128))
                    g.when(cond, go)
            elif kind == "G":
                for dist in range(DEPTH):
                    if dist:
                        g.sibling(dist, 0, ("D",))
                    g.sibling(dist, 1, ("D",))
                feed(units - 2 * LANES, (256, 256))
            else:
                run_events(g, (tok,))
    else:
        masks()
        for j in range(nq):
            project(j)
        for j in range(nq):
            attend(j)
        norm1()
        for c in wloads:
            c.wait()

        def feed_step(s, carry):
            feed(pl.multiple_of(s * 2 * LANES, 2 * LANES), (256, 256))
            return carry

        lax.fori_loop(0, units // (2 * LANES), feed_step, 0)

    loads[5].wait()

    def norm2_rows(i, carry):
        r = pl.ds(pl.multiple_of(i * ROWB, ROWB), ROWB)
        n, rstd = normalize(hidden[r, :] + acc[r, :])
        outv[r, :] = (n * g2[...] + b2[...]).astype(BF16)
        dn = cot[r, :].astype(F32) * live[r, 0:1] * g2[...]
        grad = norm_back(dn, n, rstd)
        gr2[r, :] = grad
        glow[r, :] = grad.astype(BF16)
        return carry

    lax.fori_loop(0, slots // ROWB, norm2_rows, 0)
    out_copy = pltpu.make_async_copy(outv, out_hbm, sem_out.at[0])
    out_copy.start()

    for u in range(units // LANES):
        rows = slice(u * LANES, (u + 1) * LANES)
        gp[:, rows] = (nt(glow[...], w[1, rows, :]) * dgelu[:, rows]).astype(BF16)
    for j in range(nq):
        acc[:, cols_of(j)] = gr2[:, cols_of(j)] + nn(gp[...], w[0, :, cols_of(j)])

    def norm1_back(i, carry):
        r = pl.ds(pl.multiple_of(i * ROWB, ROWB), ROWB)
        grad = norm_back(acc[r, :] * g1[...], n1[r, :], rstd1[r, 0:1])
        gr2[r, :] = grad
        glow[r, :] = grad.astype(BF16)
        return carry

    lax.fori_loop(0, slots // ROWB, norm1_back, 0)

    for j in range(nq):
        hid_low[:, cols_of(j)] = nt(glow[...], wo[cols_of(j), :]).astype(BF16)
    ones_shape = (LANES, QUAD * PAD)
    ones = (lax.broadcasted_iota(jnp.int32, ones_shape, 0) // 64 == lax.broadcasted_iota(jnp.int32, ones_shape, 1) // PAD).astype(BF16)
    dsp, delta = [], []
    for j in range(nq):
        cols = cols_of(j)
        do = hid_low[:, cols]
        delta.append(split_dot(do.astype(F32) * mixed[:, cols], ones))
        dsp.append((ppref[j] * (nt(do, vm[j, QUAD * slots:, :]) - delta[j])).astype(BF16))
        gk = jnp.where(block_diag, nn(dsp[j].astype(F32).T.astype(BF16), q[:, cols]), 0.0)
        gv = jnp.where(block_diag, nn(ppref[j].T.astype(BF16), do), 0.0)
        part[0, :, cols] = (gk[0:32] + gk[32:64] + gk[64:96] + gk[96:128])[:HELD]
        part[1, :, cols] = (gv[0:32] + gv[32:64] + gv[64:96] + gv[96:128])[:HELD]
    if remote:
        red.step0()
    for j in range(nq):
        cols = cols_of(j)
        do = hid_low[:, cols]
        delta_t = delta[j].T
        ds[:, QUAD * slots:] = dsp[j]
        for h in range(QUAD):
            rows = slice(h * slots, (h + 1) * slots)
            vh = vm[j, rows, :]
            ds[:, rows] = (prob[j * QUAD + h] * (nt(do, vh) - delta[j][:, h * PAD:h * PAD + 1])).astype(BF16)
            ds_t[:, rows] = (prob_t[j, :, rows].astype(F32) * (nt(vh, do) - delta_t[h * PAD:h * PAD + 1, :])).astype(BF16)
        dq[:, cols] = nn(ds[...], km[j]).astype(BF16) * jnp.asarray(0.125, BF16)
        dk[:, cols] = nn(ds_t[...], qm[j]).astype(BF16)
        dom = jnp.concatenate([jnp.where(head_mask((slots, LANES), h), do, jnp.zeros((), BF16)) for h in range(QUAD)], axis=0)
        dv[:, cols] = nn(prob_t[j], dom).astype(BF16)
        if remote:
            if j == 0:
                red.step1()
            if j == 2:
                red.step2()

    out_copy.wait()
    for j in range(nq):
        cols = cols_of(j)
        grad = gr2[:, cols] + nt(dq[...], wq[cols, :]) + nt(dk[...], wk[cols, :]) + nt(dv[...], wv[cols, :])
        outv[:, cols] = grad.astype(BF16)
    done = pltpu.make_async_copy(outv, gin_hbm, sem_out.at[1])
    done.start()
    if remote:
        red.step3()
        red.step4()
        dpk_ref[...] = total[0, :PREF]
        dpv_ref[...] = total[1, :PREF]
        g.finish()
    else:
        dpk_ref[...] = part[0, :PREF]
        dpv_ref[...] = part[1, :PREF]
    done.wait()


def body(
    remote, inputs, seg_ids, w_query, w_key, w_value, w_attn_out, norm1_gain, norm1_bias, ffn_in, ffn_out, norm2_gain,
    norm2_bias, prefix_key, prefix_value, cotangent,
):
    rows, slots, width = inputs.shape
    if remote:
        fin, fout = ffn_in, ffn_out
        units = ffn_in.shape[0] * lax.axis_size("ffn")
    else:
        fin = lax.all_gather(ffn_in, "ffn", axis=0, tiled=True)
        fout = lax.all_gather(ffn_out, "ffn", axis=0, tiled=True)
        units = fin.shape[0]
    nq = width // LANES
    any_spec = pl.BlockSpec(memory_space=pl.ANY)
    vmem = pl.BlockSpec(memory_space=pltpu.VMEM)

    def run(x, seg, cot):
        def sq(n=1):
            return pltpu.VMEM((slots, n * width), BF16)

        full = pltpu.VMEM((slots, width), F32)
        wide = QUAD * slots + QUAD * PAD
        scratch = [
            sq(), sq(),
            *[pltpu.VMEM((width, width), BF16) for _ in range(4)],
            pltpu.VMEM((2, units, width), BF16),
            sq(), sq(), sq(),
            pltpu.VMEM((nq, wide, LANES), BF16),
            pltpu.VMEM((nq, QUAD * slots, LANES), BF16),
            pltpu.VMEM((nq, wide, LANES), BF16),
            pltpu.VMEM((HEADS, slots, slots), F32),
            pltpu.VMEM((nq, slots, QUAD * slots), BF16),
            pltpu.VMEM((nq, slots, QUAD * PAD), F32),
            full, sq(),
            full, pltpu.VMEM((slots, 128), F32), full, sq(),
            pltpu.VMEM((slots, units), F32),
            pltpu.VMEM((slots, units), BF16),
            full, full, sq(),
            pltpu.VMEM((slots, slots), F32),
            pltpu.VMEM((slots, 128), F32),
            pltpu.VMEM((PAD, width), F32), pltpu.VMEM((PAD, width), F32),
            pltpu.VMEM((slots, wide), BF16),
            pltpu.VMEM((slots, QUAD * slots), BF16),
            sq(), sq(), sq(), sq(),
            pltpu.SemaphoreType.DMA((6,)),
            pltpu.SemaphoreType.DMA((4,)),
            pltpu.SemaphoreType.DMA((2,)),
            pltpu.VMEM((2, HELD, width), F32),
        ]
        if remote:
            shards = lax.axis_size("ffn")
            scratch += [
                pltpu.SemaphoreType.DMA((SENDS,)),
                pltpu.SemaphoreType.DMA((shards, 7)),
                pltpu.SemaphoreType.DMA((shards, 7)),
                pltpu.VMEM((HELD, width), F32),
                pltpu.VMEM((3, HELD, LANES), F32),
                pltpu.VMEM((DEPTH, HELD, LANES), F32),
                pltpu.VMEM((2, HELD, width), F32),
                pltpu.SemaphoreType.DMA((16,)),
                pltpu.SemaphoreType.DMA((16,)),
            ]
        params = {"collective_id": 0, "has_side_effects": True} if remote else {}
        return pl.pallas_call(
            functools.partial(kernel, remote),
            out_shape=(
                jax.ShapeDtypeStruct((slots, width), BF16),
                jax.ShapeDtypeStruct((slots, width), BF16),
                jax.ShapeDtypeStruct((PREF, width), F32),
                jax.ShapeDtypeStruct((PREF, width), F32),
            ),
            in_specs=[any_spec, vmem, any_spec, any_spec, any_spec, any_spec, vmem, vmem, any_spec, any_spec, vmem, vmem,
                      vmem, vmem, any_spec],
            out_specs=(any_spec, any_spec, vmem, vmem),
            scratch_shapes=scratch,
            compiler_params=pltpu.CompilerParams(vmem_limit_bytes=63 * 2**20, **params),
        )(x, seg, w_query, w_key, w_value, w_attn_out, norm1_gain.reshape(1, width), norm1_bias.reshape(1, width),
          fin, fout, norm2_gain.reshape(1, width), norm2_bias.reshape(1, width), prefix_key, prefix_value, cot)

    parts = [run(inputs[r], seg_ids[r:r + 1], cotangent[r]) for r in range(rows)]
    out = jnp.stack([p[0] for p in parts])
    gin = jnp.stack([p[1] for p in parts])
    dpk, dpv = parts[0][2:]
    if not remote:
        dpk, dpv = lax.psum((sum(p[2] for p in parts), sum(p[3] for p in parts)), ("dp", "ffn"))
    return out, gin, dpk, dpv


def solution(mesh):
    row = P(("dp", "ffn"), None, None)
    remote = mesh.shape["ffn"] == 2 * DEPTH and mesh.shape["dp"] == 4
    return jax.shard_map(
        functools.partial(body, remote),
        mesh=mesh,
        in_specs=(row, P(("dp", "ffn"), None), P(), P(), P(), P(), P(), P(), P("ffn", None), P("ffn", None), P(), P(),
                  P(), P(), row),
        out_specs=(row, row, P(), P()),
        check_vma=False,
    )
```

```python
import functools

import jax
import jax.numpy as jnp
from jax import lax
from jax.experimental import pallas as pl
from jax.experimental.pallas import tpu as pltpu
from jax.sharding import PartitionSpec as P

HEADS = 16
PREF = 20
PAIRS = 7
EPS = 1e-05
NEG = -1e30
QUAD = 4
LANES = 256
PAD = 32
HELD = 24
ROWB = 16
UNROLL = 4
F32 = jnp.float32
BF16 = jnp.bfloat16


def nt(a, b):
    return lax.dot_general(a, b, (((1,), (1,)), ((), ())), preferred_element_type=F32)


def nn(a, b):
    return lax.dot_general(a, b, (((1,), (0,)), ((), ())), preferred_element_type=F32)


def head_mask(shape, h):
    return lax.broadcasted_iota(jnp.int32, shape, 1) // 64 == h


def normalize(r):
    center = r - jnp.mean(r, axis=-1, keepdims=True)
    spread = jnp.mean(center * center, axis=-1, keepdims=True)
    rstd = lax.rsqrt(spread + EPS)
    return center * rstd, rstd


def norm_back(dn, n, rstd):
    return rstd * (dn - jnp.mean(dn, axis=-1, keepdims=True) - n * jnp.mean(dn * n, axis=-1, keepdims=True))


def split_dot(a, ones):
    hi = a.astype(BF16)
    return nn(hi, ones) + nn((a - hi.astype(F32)).astype(BF16), ones)


def gelu_parts(pre):
    cdf = 0.5 * (1.0 + lax.erf(pre * 0.7071067811865476))
    return pre * cdf, cdf + pre * (0.3989422804014327 * jnp.exp(-0.5 * pre * pre))


MESH_ID = pl.DeviceIdType.MESH
DEPTH = 4
LINKS = ("x", "y", "core", 1, -1)
PART_ROWS = (64, 64, 80, 80, 80, 80, 64)
PART_OFF = (0, 64, 128, 208, 288, 368, 448)
MAIN = 448
FAR = 64
A0, A1, B0, B1, C0, C1, DD = range(7)


class Gather:
    def __init__(self, w, shards, ssem, rsem, bsem):
        self.w, self.shards, self.ssem, self.rsem, self.bsem = w, shards, ssem, rsem, bsem
        d, f = lax.axis_index("dp"), lax.axis_index("ffn")
        self.y, self.c = d // 2, lax.rem(d, 2)
        self.z, self.x = f // 2, lax.rem(f, 2)
        self.sent = []
        self.dev = {
            "core": (self.y * 2 + 1 - self.c, f),
            "y": ((1 - self.y) * 2 + self.c, f),
            "x": (d, self.z * 2 + 1 - self.x),
            1: (d, jnp.minimum(self.z + 1, DEPTH - 1) * 2 + self.x),
            -1: (d, jnp.maximum(self.z - 1, 0) * 2 + self.x),
        }
        self.can = {1: lambda: self.z < DEPTH - 1, -1: lambda: self.z > 0, "x": None, "y": None, "core": None}

    def part(self, name):
        if name[0] in "PO":
            plane = self.y if name[0] == "P" else 1 - self.y
            i = int(name[1])
            return pl.multiple_of(PART_OFF[B0 + i] + plane * 160, 16), 80, B0 + i + 2 * plane
        i = {"A0": A0, "A1": A1, "D": DD}[name]
        return PART_OFF[i], PART_ROWS[i], i

    def place(self, m, s, off, rows, num):
        if isinstance(num, int) and num == DD:
            start = self.shards * MAIN + s * FAR
        else:
            start = s * MAIN + off
        return self.w.at[m, pl.ds(pl.multiple_of(start, 16), rows)]

    def copy(self, to, s, part):
        off, rows, num = part
        ref = self.place(self.c, s, off, rows, num)
        if to == "core":
            recv = self.bsem.at[self.shards if isinstance(num, int) and num == DD else s]
        else:
            recv = self.rsem.at[s, num]
        return pltpu.make_async_remote_copy(
            src_ref=ref, dst_ref=ref, send_sem=self.ssem.at[LINKS.index(to)], recv_sem=recv, device_id=self.dev[to],
            device_id_type=MESH_ID,
        )

    def start(self, to, s, name):
        self.copy(to, s, self.part(name)).start()

    def send(self, to, s, name):
        desc = self.copy(to, s, self.part(name))
        can = self.can[to]
        if can is None:
            desc.start()
        else:
            pl.when(can())(desc.start)

    def when(self, cond, fn):
        if cond is None:
            fn()
        else:
            pl.when(cond())(fn)

    def shard(self, dz, column):
        return jnp.clip(self.z + dz, 0, DEPTH - 1) * 2 + (self.x if column == 0 else 1 - self.x)

    def wait(self, s, name):
        self.copy("x", s, self.part(name)).wait_recv()

    def step(self, k):
        if k == 0:
            return [(0, None, 0)]
        if k == 1:
            return [(1, self.can[1], 1), (-1, self.can[-1], -1)]
        dz = jnp.where(self.z < DEPTH // 2, k, -k)
        if k == 2:
            return [(dz, None, None)]
        return [(dz, lambda: jnp.logical_or(self.z == 0, self.z == DEPTH - 1), None)]

    def along(self, dz, sign, s, name):
        if sign is None:
            pl.when(self.z == 1)(lambda: self.start(-1, s, name))
            pl.when(self.z == DEPTH - 2)(lambda: self.start(1, s, name))
        elif sign:
            self.send(-sign, s, name)

    def from_z(self, k, name):
        for dz, cond, sign in self.step(k):
            def go(dz=dz, sign=sign):
                s = self.shard(dz, 0)
                self.wait(s, name)
                if k < 3:
                    self.along(dz, sign, s, name)
                if name[0] == "P":
                    self.send("y", s, name)
                self.send("x", s, name)
                self.send("core", s, name)
            self.when(cond, go)

    def from_x(self, k, name):
        for dz, cond, sign in self.step(k):
            def go(dz=dz):
                s = self.shard(dz, 1)
                self.wait(s, name)
                if name[0] == "P":
                    self.send("y", s, name)
                if name == "D":
                    self.send(1, s, name)
                    self.send(-1, s, name)
                self.send("core", s, name)
            self.when(cond, go)

    def far(self, k, column):
        for dz, cond, sign in self.step(k):
            def go(dz=dz, sign=sign):
                s = self.shard(dz, column)
                self.wait(s, "D")
                if k < 3:
                    self.along(dz, sign, s, "D")
                self.send("core", s, "D")
            self.when(cond, go)

    def from_y(self, k, column, name):
        for dz, cond, sign in self.step(k):
            def go(dz=dz):
                s = self.shard(dz, column)
                self.wait(s, name)
                self.send("core", s, name)
            self.when(cond, go)

    def sibling(self, k, column):
        for dz, cond, sign in self.step(k):
            def go(dz=dz):
                s = self.shard(dz, column)
                self.await_rows(self.place(1 - self.c, s, 0, MAIN, 0), self.bsem.at[s], False)
            self.when(cond, go)

    def await_rows(self, ref, sem, sent):
        desc = pltpu.make_async_remote_copy(
            src_ref=ref, dst_ref=ref, send_sem=sem, recv_sem=sem, device_id=self.dev["core"], device_id_type=MESH_ID
        )
        if sent:
            desc.wait_send()
        else:
            desc.wait_recv()

    def sibling_far(self):
        self.await_rows(self.w.at[1 - self.c, pl.ds(0, (self.shards - 1) * FAR)], self.bsem.at[self.shards], False)

    def meet(self):
        bar = pltpu.get_barrier_semaphore()
        for to in LINKS:
            def hello(to=to):
                pl.semaphore_signal(bar, inc=1, device_id=self.dev[to], device_id_type=MESH_ID)
            self.when(self.can[to], hello)
        pl.semaphore_wait(bar, 3 + (self.z > 0).astype(jnp.int32) + (self.z < DEPTH - 1).astype(jnp.int32))

    def finish(self):
        plane = MAIN - 160
        for i, to in enumerate(LINKS):
            if to in (1, -1):
                for z in range(DEPTH):
                    depth = (z + 1 if to == 1 else DEPTH - z) * (plane + 2 * FAR)
                    if 0 <= z + to < DEPTH:
                        def done(depth=depth, i=i):
                            self.await_rows(self.w.at[0, pl.ds(0, depth)], self.ssem.at[i], True)
                        pl.when(self.z == z)(done)
            else:
                rows = {"x": DEPTH * plane + FAR, "y": (self.shards - 1) * 160, "core": (self.shards - 1) * (MAIN + FAR)}[to]
                self.await_rows(self.w.at[0, pl.ds(0, rows)], self.ssem.at[i], True)

    def local(self, fin, fout, sem):
        s = self.shard(0, 0)
        out = []
        for m, src in enumerate((fin, fout)):
            out.append(pltpu.make_async_copy(src.at[pl.ds(0, MAIN)], self.place(m, s, 0, MAIN, 0), sem.at[2 * m]))
            out.append(pltpu.make_async_copy(src.at[pl.ds(MAIN, FAR)], self.place(m, s, MAIN, FAR, DD), sem.at[2 * m + 1]))
        for c in out:
            c.start()
        return out


def run_events(g, toks):
    for ev in toks:
        kind, k, name = ev[0], ev[1], ev[2:]
        if kind == "s":
            for to in ("x",) if k == "x" else (1, -1):
                g.send(to, g.shard(0, 0), ev[3:])
        elif kind == "z":
            g.from_z(int(k), name)
        elif kind == "x":
            g.from_x(int(k), name)
        elif kind in "de":
            g.far(int(k), int(kind == "e"))
        elif kind in "Yy":
            g.from_y(int(k), int(kind == "y"), name)


ORDER = (
    "sx:P1", "sz:P1", "sx:A0", "sz:P0", "x0P1", "sx:P0", "sx:A1", "z1P1", "sx:D", "CM", "z1P0", "sz:D", "x0P0", "CQ0", "x0A1", "sz:A1", "z2P0", "sz:A0", "y0O1",
    "z2P1", "CQ1", "x0D", "CQ2", "CQ3", "x1P1", "z3P0", "z1A1", "z3P1", "z1A0", "x0A0", "CA0", "e1", "Y1O0", "x3P0", "z2A1", "y0O0", "x1P0", "CA1", "CA2", "Y3O0", "Y2O1",
    "CA3", "CL", "y3O0", "d1", "x2P1", "x2P0", "z2A0", "Y1O1", "F0", "y1O1", "x1A1", "y1O0", "x1A0", "z3A1", "Y2O0", "e2", "d2", "x3P1", "F1", "x2A0", "Y3O1", "y2O1",
    "x2A1", "z3A0", "y2O0", "x3A1", "F2", "x3A0", "y3O1", "d3", "e3", "F3", "G",
)


class Reduce:
    def __init__(self, g, part, got, along, total, ssem, rsem):
        self.g, self.part, self.got, self.along, self.total, self.ssem, self.rsem = g, part, got, along, total, ssem, rsem
        y, x, z, c = g.y, g.x, g.z, g.c
        self.mine = (y * 2 + x) * 2 + c
        spots = [
            (yy, xx, cc) for cc in (1 - c, c) for yy, xx in ((1 - y, 1 - x), (1 - y, x), (y, 1 - x), (y, x))
        ][:7]
        self.mates = [((yy * 2 + xx) * 2 + cc, (yy * 2 + cc, z * 2 + xx)) for yy, xx, cc in spots]
        self.far_z = [(lax.rem(z + i, DEPTH), (y * 2 + c, lax.rem(z + i, DEPTH) * 2 + x)) for i in range(1, DEPTH)]

    def copy(self, src, dst, stage, recv, dev):
        return pltpu.make_async_remote_copy(
            src_ref=src, dst_ref=dst, send_sem=self.ssem.at[stage], recv_sem=self.rsem.at[stage, recv], device_id=dev,
            device_id_type=MESH_ID,
        )

    def scatter(self):
        for owner, dev in self.mates:
            self.copy(self.part.at[owner], self.got.at[self.mine], 0, self.mine, dev).start()

    def along_z(self):
        for owner, dev in self.mates:
            self.copy(self.part.at[owner], self.got.at[owner], 0, owner, dev).wait_recv()
        self.got[self.mine] = self.part[self.mine]
        parts = [self.got[i].astype(F32) for i in range(8)]
        z = self.g.z
        self.along[z] = (
            ((parts[0] + parts[1]) + (parts[2] + parts[3])) + ((parts[4] + parts[5]) + (parts[6] + parts[7]))
        ).astype(BF16)
        for zz, dev in self.far_z:
            self.copy(self.along.at[z], self.along.at[z], 1, z, dev).start()

    def spread(self):
        for zz, dev in self.far_z:
            self.copy(self.along.at[zz], self.along.at[zz], 1, zz, dev).wait_recv()
        rows = [self.along[i].astype(F32) for i in range(DEPTH)]
        self.total[self.mine] = ((rows[0] + rows[1]) + (rows[2] + rows[3])).astype(BF16)
        for owner, dev in self.mates:
            self.copy(self.total.at[self.mine], self.total.at[self.mine], 2, self.mine, dev).start()

    def collect(self, dpk_ref, dpv_ref):
        for owner, dev in self.mates:
            self.copy(self.total.at[owner], self.total.at[owner], 2, owner, dev).wait_recv()
        for i in range(8):
            both = self.total[i].astype(F32)
            dpk_ref[:, i * 128:(i + 1) * 128] = both[:PREF]
            dpv_ref[:, i * 128:(i + 1) * 128] = both[HELD:HELD + PREF]

    def finish(self):
        for stage, n in enumerate((7, DEPTH - 1, 7)):
            ref = self.got.at[pl.ds(0, n)]
            self.copy(ref, ref, stage, 0, self.g.dev["core"]).wait_send()


def kernel(
    remote,
    x_hbm, seg_ref, wq_hbm, wk_hbm, wv_hbm, wo_hbm, g1, b1, fin_hbm, fout_hbm, g2, b2, pk_ref, pv_ref, cot_hbm,
    out_hbm, gin_hbm, dpk_ref, dpv_ref,
    x, cot, wq, wk, wv, wo, w, q, k, v, km, qm, vm, prob, prob_t, ppref, mixed, mixed_low, n1, rstd1, hidden, hid_low,
    dgelu, gp, acc, gr2, glow, bias, live, pad_k, pad_v, ds, ds_t, outv, dq, dk, dv, sem_in, sem_w, sem_out,
    part, *comm,
):
    slots, width = x.shape
    units = w.shape[1]
    nq = width // LANES
    srcs = [(x_hbm, x), (wq_hbm, wq), (wk_hbm, wk), (wv_hbm, wv), (wo_hbm, wo), (cot_hbm, cot)]
    loads = [pltpu.make_async_copy(s, d, sem_in.at[i]) for i, (s, d) in enumerate(srcs)]
    if remote:
        ssem, rsem, bsem, got, along, total, red_s, red_r = comm
        g = Gather(w, units // (MAIN + FAR), ssem, rsem, bsem)
        red = Reduce(g, part, got, along, total, red_s, red_r)
        wloads = g.local(fin_hbm, fout_hbm, sem_w)
    else:
        wloads = [pltpu.make_async_copy(src, w.at[m], sem_w.at[m]) for m, src in enumerate((fin_hbm, fout_hbm))]
    for c in loads[:4]:
        c.start()
    if not remote:
        for c in wloads:
            c.start()
    for c in loads[4:]:
        c.start()
    bd_shape = (QUAD * PAD, LANES)
    block_diag = lax.broadcasted_iota(jnp.int32, bd_shape, 0) // PAD == lax.broadcasted_iota(jnp.int32, bd_shape, 1) // 64
    lane = lax.broadcasted_iota(jnp.int32, (1, QUAD * PAD), 1)

    def cols_of(j):
        return slice(j * LANES, (j + 1) * LANES)

    def pref_bias(h):
        return jnp.where((lane // PAD == h) & (lane % PAD < PREF), 0.0, NEG)

    def block(ref, j):
        part = ref[:, cols_of(j)]
        return jnp.where(block_diag, jnp.concatenate([part] * QUAD, axis=0), 0.0).astype(BF16)

    def masks():
        seg_row = jnp.broadcast_to(seg_ref[...].astype(F32), (slots, slots))
        seg_col = seg_row.T
        bias[...] = jnp.where((seg_row == seg_col) & (seg_row < PAIRS), 0.0, NEG)
        live[...] = (seg_col[:, :128] < PAIRS).astype(F32)
        pad_k[...] = jnp.zeros_like(pad_k)
        pad_v[...] = jnp.zeros_like(pad_v)
        pad_k[0:PREF, :] = pk_ref[...]
        pad_v[0:PREF, :] = pv_ref[...]

    def project(j):
        cols = cols_of(j)
        if j == 0:
            for i in range(4):
                loads[i].wait()
        q[:, cols] = (nn(x[...], wq[:, cols]) * 0.125).astype(BF16)
        k[:, cols] = nn(x[...], wk[:, cols]).astype(BF16)
        v[:, cols] = nn(x[...], wv[:, cols]).astype(BF16)
        for h in range(QUAD):
            rows = slice(h * slots, (h + 1) * slots)
            keep = head_mask((slots, LANES), h)
            qm[j, rows, :] = jnp.where(keep, q[:, cols], jnp.zeros((), BF16))
            km[j, rows, :] = jnp.where(keep, k[:, cols], jnp.zeros((), BF16))
            vm[j, rows, :] = jnp.where(keep, v[:, cols], jnp.zeros((), BF16))
        km[j, QUAD * slots:, :] = block(pad_k, j)
        vm[j, QUAD * slots:, :] = block(pad_v, j)

    def attend(j):
        cols = cols_of(j)
        sp_all = nt(q[:, cols], km[j, QUAD * slots:, :])
        pp_all = jnp.zeros((slots, QUAD * PAD), F32)
        for h in range(QUAD):
            rows = slice(h * slots, (h + 1) * slots)
            s = nt(q[:, cols], km[j, rows, :]) + bias[...]
            sp = sp_all + pref_bias(h)
            top = jnp.maximum(jnp.max(s, axis=-1, keepdims=True), jnp.max(sp, axis=-1, keepdims=True))
            e = jnp.exp(s - top)
            ep = jnp.exp(sp - top)
            inv = 1.0 / (jnp.sum(e, axis=-1, keepdims=True) + jnp.sum(ep, axis=-1, keepdims=True))
            p = e * inv
            prob[j * QUAD + h] = p
            ds[:, rows] = p.astype(BF16)
            prob_t[j, :, rows] = p.T.astype(BF16)
            pp_all = pp_all + ep * inv
        ppref[j] = pp_all
        ds[:, QUAD * slots:] = pp_all.astype(BF16)
        o = nn(ds[...], vm[j])
        mixed[:, cols] = o
        mixed_low[:, cols] = o.astype(BF16)

    def norm1():
        loads[4].wait()
        for j in range(nq):
            acc[:, cols_of(j)] = nn(mixed_low[...], wo[:, cols_of(j)])

        def rows_of(i, carry):
            r = pl.ds(pl.multiple_of(i * ROWB, ROWB), ROWB)
            n, rstd = normalize(x[r, :].astype(F32) + acc[r, :])
            n1[r, :] = n
            rstd1[r, :] = jnp.broadcast_to(rstd, (ROWB, 128))
            h = n * g1[...] + b1[...]
            hidden[r, :] = h
            hid_low[r, :] = h.astype(BF16)
            acc[r, :] = jnp.zeros((ROWB, width), F32)
            return carry

        lax.fori_loop(0, slots // ROWB, rows_of, 0, unroll=UNROLL)

    def feed(base, sizes):
        at, total = 0, sum(sizes)
        for n in sizes:
            act, slope = gelu_parts(nt(hid_low[...], w[0, pl.ds(base + at, n), :]))
            dgelu[:, pl.ds(base + at, n)] = slope
            gp[:, at:at + n] = act.astype(BF16)
            at += n
        for j in range(nq):
            acc[:, cols_of(j)] += nn(gp[:, :total], w[1, pl.ds(base, total), cols_of(j)])

    if remote:
        g.meet()
        for c in wloads:
            c.wait()
        pair = 2 * MAIN
        for tok in ORDER:
            kind = tok[0]
            if kind == "C":
                step = tok[1:]
                if step == "M":
                    masks()
                elif step == "L":
                    norm1()
                elif step[0] == "Q":
                    project(int(step[1]))
                else:
                    attend(int(step[1]))
            elif kind == "F":
                dist = int(tok[1])
                if dist:
                    g.sibling(dist, 0)
                g.sibling(dist, 1)
                for dz, cond, sign in g.step(dist):
                    def go(dz=dz):
                        where = jnp.clip(g.z + dz, 0, DEPTH - 1)
                        feed(pl.multiple_of(where * pair, 128), (256, 256, 256, 128))
                    g.when(cond, go)
            elif kind == "G":
                g.sibling_far()
                feed(units - 2 * LANES, (256, 256))
            else:
                run_events(g, (tok,))
    else:
        masks()
        for j in range(nq):
            project(j)
        for j in range(nq):
            attend(j)
        norm1()
        for c in wloads:
            c.wait()

        def feed_step(s, carry):
            feed(pl.multiple_of(s * 2 * LANES, 2 * LANES), (256, 256))
            return carry

        lax.fori_loop(0, units // (2 * LANES), feed_step, 0)

    loads[5].wait()

    def norm2_rows(i, carry):
        r = pl.ds(pl.multiple_of(i * ROWB, ROWB), ROWB)
        n, rstd = normalize(hidden[r, :] + acc[r, :])
        (out_hbm if remote else outv)[r, :] = (n * g2[...] + b2[...]).astype(BF16)
        dn = cot[r, :].astype(F32) * live[r, 0:1] * g2[...]
        grad = norm_back(dn, n, rstd)
        gr2[r, :] = grad
        glow[r, :] = grad.astype(BF16)
        return carry

    lax.fori_loop(0, slots // ROWB, norm2_rows, 0, unroll=UNROLL)
    if not remote:
        out_copy = pltpu.make_async_copy(outv, out_hbm, sem_out.at[0])
        out_copy.start()

    for u in range(units // LANES):
        rows = slice(u * LANES, (u + 1) * LANES)
        gp[:, rows] = (nt(glow[...], w[1, rows, :]) * dgelu[:, rows]).astype(BF16)
    for j in range(nq):
        acc[:, cols_of(j)] = gr2[:, cols_of(j)] + nn(gp[...], w[0, :, cols_of(j)])

    def norm1_back(i, carry):
        r = pl.ds(pl.multiple_of(i * ROWB, ROWB), ROWB)
        grad = norm_back(acc[r, :] * g1[...], n1[r, :], rstd1[r, 0:1])
        gr2[r, :] = grad
        glow[r, :] = grad.astype(BF16)
        return carry

    lax.fori_loop(0, slots // ROWB, norm1_back, 0, unroll=UNROLL)

    for j in range(nq):
        hid_low[:, cols_of(j)] = nt(glow[...], wo[cols_of(j), :]).astype(BF16)
    ones_shape = (LANES, QUAD * PAD)
    ones = (lax.broadcasted_iota(jnp.int32, ones_shape, 0) // 64 == lax.broadcasted_iota(jnp.int32, ones_shape, 1) // PAD).astype(BF16)
    dsp, delta = [], []
    for j in range(nq):
        cols = cols_of(j)
        do = hid_low[:, cols]
        delta.append(split_dot(do.astype(F32) * mixed[:, cols], ones))
        dsp.append((ppref[j] * (nt(do, vm[j, QUAD * slots:, :]) - delta[j])).astype(BF16))
        gk = jnp.where(block_diag, nn(dsp[j].astype(F32).T.astype(BF16), q[:, cols]), 0.0)
        gv = jnp.where(block_diag, nn(ppref[j].T.astype(BF16), do), 0.0)
        both = jnp.concatenate([sum(t[i * PAD:i * PAD + HELD] for i in range(QUAD)) for t in (gk, gv)], axis=0)
        for i in range(2):
            part[2 * j + i] = both[:, i * 128:(i + 1) * 128].astype(part.dtype)
    if remote:
        red.scatter()
    for j in range(nq):
        cols = cols_of(j)
        do = hid_low[:, cols]
        delta_t = delta[j].T
        ds[:, QUAD * slots:] = dsp[j]
        for h in range(QUAD):
            rows = slice(h * slots, (h + 1) * slots)
            vh = vm[j, rows, :]
            ds[:, rows] = (prob[j * QUAD + h] * (nt(do, vh) - delta[j][:, h * PAD:h * PAD + 1])).astype(BF16)
            ds_t[:, rows] = (prob_t[j, :, rows].astype(F32) * (nt(vh, do) - delta_t[h * PAD:h * PAD + 1, :])).astype(BF16)
        dq[:, cols] = nn(ds[...], km[j]).astype(BF16) * jnp.asarray(0.125, BF16)
        dk[:, cols] = nn(ds_t[...], qm[j]).astype(BF16)
        dom = jnp.concatenate([jnp.where(head_mask((slots, LANES), h), do, jnp.zeros((), BF16)) for h in range(QUAD)], axis=0)
        dv[:, cols] = nn(prob_t[j], dom).astype(BF16)
        if remote and j == 0:
            g.finish()
        if remote and j == 2:
            red.along_z()

    if not remote:
        out_copy.wait()
    for j in range(nq):
        cols = cols_of(j)
        grad = gr2[:, cols] + nt(dq[...], wq[cols, :]) + nt(dk[...], wk[cols, :]) + nt(dv[...], wv[cols, :])
        (gin_hbm if remote else outv)[:, cols] = grad.astype(BF16)
        if remote and j == 1:
            red.spread()
    if remote:
        red.collect(dpk_ref, dpv_ref)
        red.finish()
    else:
        for i in range(8):
            dpk_ref[:, i * 128:(i + 1) * 128] = part[i, :PREF]
            dpv_ref[:, i * 128:(i + 1) * 128] = part[i, HELD:HELD + PREF]
        done = pltpu.make_async_copy(outv, gin_hbm, sem_out.at[1])
        done.start()
        done.wait()


def settle(*refs):
    half = len(refs) // 2
    copies = [pltpu.make_async_copy(refs[i], refs[half + i], refs[-1].at[i]) for i in range(half)]
    for c in copies:
        c.start()
    for c in copies:
        c.wait()


def body(
    remote, inputs, seg_ids, w_query, w_key, w_value, w_attn_out, norm1_gain, norm1_bias, ffn_in, ffn_out, norm2_gain,
    norm2_bias, prefix_key, prefix_value, cotangent,
):
    rows, slots, width = inputs.shape
    if remote:
        fin, fout = ffn_in, ffn_out
        units = ffn_in.shape[0] * lax.axis_size("ffn")
    else:
        fin = lax.all_gather(ffn_in, "ffn", axis=0, tiled=True)
        fout = lax.all_gather(ffn_out, "ffn", axis=0, tiled=True)
        units = fin.shape[0]
    nq = width // LANES
    any_spec = pl.BlockSpec(memory_space=pl.ANY)
    vmem = pl.BlockSpec(memory_space=pltpu.VMEM)

    def run(x, seg, cot):
        def sq(n=1):
            return pltpu.VMEM((slots, n * width), BF16)

        full = pltpu.VMEM((slots, width), F32)
        wide = QUAD * slots + QUAD * PAD
        scratch = [
            sq(), sq(),
            *[pltpu.VMEM((width, width), BF16) for _ in range(4)],
            pltpu.VMEM((2, units, width), BF16),
            sq(), sq(), sq(),
            pltpu.VMEM((nq, wide, LANES), BF16),
            pltpu.VMEM((nq, QUAD * slots, LANES), BF16),
            pltpu.VMEM((nq, wide, LANES), BF16),
            pltpu.VMEM((HEADS, slots, slots), F32),
            pltpu.VMEM((nq, slots, QUAD * slots), BF16),
            pltpu.VMEM((nq, slots, QUAD * PAD), F32),
            full, sq(),
            full, pltpu.VMEM((slots, 128), F32), full, sq(),
            pltpu.VMEM((slots, units), F32),
            pltpu.VMEM((slots, units), BF16),
            full, full, sq(),
            pltpu.VMEM((slots, slots), F32),
            pltpu.VMEM((slots, 128), F32),
            pltpu.VMEM((PAD, width), F32), pltpu.VMEM((PAD, width), F32),
            pltpu.VMEM((slots, wide), BF16),
            pltpu.VMEM((slots, QUAD * slots), BF16),
            sq(), sq(), sq(), sq(),
            pltpu.SemaphoreType.DMA((6,)),
            pltpu.SemaphoreType.DMA((4,)),
            pltpu.SemaphoreType.DMA((2,)),
            pltpu.VMEM((8, 2 * HELD, 128), BF16 if remote else F32),
        ]
        if remote:
            shards = lax.axis_size("ffn")
            scratch += [
                pltpu.SemaphoreType.DMA((len(LINKS),)),
                pltpu.SemaphoreType.DMA((shards, 7)),
                pltpu.SemaphoreType.DMA((shards + 1,)),
                pltpu.VMEM((8, 2 * HELD, 128), BF16),
                pltpu.VMEM((DEPTH, 2 * HELD, 128), BF16),
                pltpu.VMEM((8, 2 * HELD, 128), BF16),
                pltpu.SemaphoreType.DMA((3,)),
                pltpu.SemaphoreType.DMA((3, 8)),
            ]
        outs = (((slots, width), BF16), ((slots, width), BF16), ((PREF, width), F32), ((PREF, width), F32))
        params = {"collective_id": 0, "has_side_effects": True} if remote else {}
        return pl.pallas_call(
            functools.partial(kernel, remote),
            out_shape=tuple((pltpu.VMEM if remote else jax.ShapeDtypeStruct)(*t) for t in outs),
            in_specs=[any_spec, vmem, any_spec, any_spec, any_spec, any_spec, vmem, vmem, any_spec, any_spec, vmem, vmem,
                      vmem, vmem, any_spec],
            out_specs=(vmem,) * 4 if remote else (any_spec, any_spec, vmem, vmem),
            scratch_shapes=scratch,
            compiler_params=pltpu.CompilerParams(vmem_limit_bytes=60 * 2**20, **params),
        )(x, seg, w_query, w_key, w_value, w_attn_out, norm1_gain.reshape(1, width), norm1_bias.reshape(1, width),
          fin, fout, norm2_gain.reshape(1, width), norm2_bias.reshape(1, width), prefix_key, prefix_value, cot)

    if remote and rows == 1:
        made = [jnp.expand_dims(t, 0) if i < 2 else t for i, t in enumerate(run(inputs[0], seg_ids, cotangent[0]))]
        return pl.pallas_call(
            settle,
            out_shape=[jax.ShapeDtypeStruct(t.shape, t.dtype) for t in made],
            in_specs=[vmem] * 4,
            out_specs=[any_spec] * 4,
            scratch_shapes=[pltpu.SemaphoreType.DMA((4,))],
            compiler_params=pltpu.CompilerParams(vmem_limit_bytes=2**20),
        )(*made)
    parts = [run(inputs[r], seg_ids[r:r + 1], cotangent[r]) for r in range(rows)]
    out = jnp.stack([p[0] for p in parts])
    gin = jnp.stack([p[1] for p in parts])
    dpk, dpv = parts[0][2:]
    if not remote:
        dpk, dpv = lax.psum((sum(p[2] for p in parts), sum(p[3] for p in parts)), ("dp", "ffn"))
    return out, gin, dpk, dpv


def solution(mesh):
    row = P(("dp", "ffn"), None, None)
    remote = mesh.shape["ffn"] == 2 * DEPTH and mesh.shape["dp"] == 4
    return jax.shard_map(
        functools.partial(body, remote),
        mesh=mesh,
        in_specs=(row, P(("dp", "ffn"), None), P(), P(), P(), P(), P(), P(), P("ffn", None), P("ffn", None), P(), P(),
                  P(), P(), row),
        out_specs=(row, row, P(), P()),
        check_vma=False,
    )
```

```python
import functools

import jax
import jax.numpy as jnp
from jax import lax
from jax.experimental import pallas as pl
from jax.experimental.pallas import tpu as pltpu
from jax.sharding import PartitionSpec as P

HEADS = 16
PREF = 20
PAIRS = 7
EPS = 1e-05
NEG = -1e30
QUAD = 4
LANES = 256
PAD = 32
HELD = 24
ROWB = 16
UNROLL = 4
F32 = jnp.float32
BF16 = jnp.bfloat16


def nt(a, b):
    return lax.dot_general(a, b, (((1,), (1,)), ((), ())), preferred_element_type=F32)


def nn(a, b):
    return lax.dot_general(a, b, (((1,), (0,)), ((), ())), preferred_element_type=F32)


def head_mask(shape, h):
    return lax.broadcasted_iota(jnp.int32, shape, 1) // 64 == h


def normalize(r):
    center = r - jnp.mean(r, axis=-1, keepdims=True)
    spread = jnp.mean(center * center, axis=-1, keepdims=True)
    rstd = lax.rsqrt(spread + EPS)
    return center * rstd, rstd


def norm_back(dn, n, rstd):
    return rstd * (dn - jnp.mean(dn, axis=-1, keepdims=True) - n * jnp.mean(dn * n, axis=-1, keepdims=True))


def gelu_parts(pre):
    cdf = 0.5 * (1.0 + lax.erf(pre * 0.7071067811865476))
    return pre * cdf, cdf + pre * (0.3989422804014327 * jnp.exp(-0.5 * pre * pre))


MESH_ID = pl.DeviceIdType.MESH
DEPTH = 4
LINKS = ("x", "y", "core", 1, -1)
PARTS = {"A0": 64, "A1": 64, "P0": 80, "P1": 80}
MAIN = 448
FAR = 64
A0, A1, B0, B1, C0, C1, DD = range(7)


class Gather:
    def __init__(self, w, shards, ssem, rsem, bsem):
        self.w, self.shards, self.ssem, self.rsem, self.bsem = w, shards, ssem, rsem, bsem
        d, f = lax.axis_index("dp"), lax.axis_index("ffn")
        self.y, self.c = d // 2, lax.rem(d, 2)
        self.z, self.x = f // 2, lax.rem(f, 2)
        self.dev = {
            "core": (self.y * 2 + 1 - self.c, f),
            "y": ((1 - self.y) * 2 + self.c, f),
            "x": (d, self.z * 2 + 1 - self.x),
            1: (d, jnp.minimum(self.z + 1, DEPTH - 1) * 2 + self.x),
            -1: (d, jnp.maximum(self.z - 1, 0) * 2 + self.x),
        }
        self.can = {1: lambda: self.z < DEPTH - 1, -1: lambda: self.z > 0, "x": None, "y": None, "core": None}

    def part(self, name):
        rows = PARTS
        if name == "D":
            return MAIN, FAR, DD
        if name[0] == "A":
            return rows["A0"] * int(name[1]), rows[name], int(name[1])
        plane = self.y if name[0] == "P" else 1 - self.y
        i = int(name[1])
        off = rows["A0"] + rows["A1"] + rows["P0"] * i + plane * self.handed()
        return pl.multiple_of(off, 16), rows["P%d" % i], B0 + i + 2 * plane

    def handed(self):
        return PARTS["P0"] + PARTS["P1"]

    def place(self, m, s, off, rows, num):
        if isinstance(num, int) and num == DD:
            start = self.shards * MAIN + s * FAR
        else:
            start = s * MAIN + off
        return self.w.at[m, pl.ds(pl.multiple_of(start, 16), rows)]

    def copy(self, to, s, part):
        off, rows, num = part
        ref = self.place(self.c, s, off, rows, num)
        if to == "core":
            far = isinstance(num, int) and num == DD
            recv = self.bsem.at[self.shards + s // DEPTH if far else s]
        else:
            recv = self.rsem.at[s, num]
        return pltpu.make_async_remote_copy(
            src_ref=ref, dst_ref=ref, send_sem=self.ssem.at[LINKS.index(to)], recv_sem=recv, device_id=self.dev[to],
            device_id_type=MESH_ID,
        )

    def start(self, to, s, name):
        self.copy(to, s, self.part(name)).start()

    def send(self, to, s, name):
        desc = self.copy(to, s, self.part(name))
        can = self.can[to]
        if can is None:
            desc.start()
        else:
            pl.when(can())(desc.start)

    def when(self, cond, fn):
        if cond is None:
            fn()
        else:
            pl.when(cond())(fn)

    def shard(self, dz, column):
        return jnp.clip(self.z + dz, 0, DEPTH - 1) * 2 + (self.x if column == 0 else 1 - self.x)

    def wait(self, s, name):
        self.copy("x", s, self.part(name)).wait_recv()

    def step(self, k):
        if k == 0:
            return [(0, None, 0)]
        if k == 1:
            return [(1, self.can[1], 1), (-1, self.can[-1], -1)]
        dz = jnp.where(self.z < DEPTH // 2, k, -k)
        if k == 2:
            return [(dz, None, None)]
        return [(dz, lambda: jnp.logical_or(self.z == 0, self.z == DEPTH - 1), None)]

    def along(self, dz, sign, s, name):
        if sign is None:
            pl.when(self.z == 1)(lambda: self.start(-1, s, name))
            pl.when(self.z == DEPTH - 2)(lambda: self.start(1, s, name))
        elif sign:
            self.send(-sign, s, name)

    def from_z(self, k, name):
        for dz, cond, sign in self.step(k):
            def go(dz=dz, sign=sign):
                s = self.shard(dz, 0)
                self.wait(s, name)
                if k < 3:
                    self.along(dz, sign, s, name)
                if name[0] == "P":
                    self.send("y", s, name)
                self.send("x", s, name)
                self.send("core", s, name)
            self.when(cond, go)

    def from_x(self, k, name):
        for dz, cond, sign in self.step(k):
            def go(dz=dz):
                s = self.shard(dz, 1)
                self.wait(s, name)
                if name[0] == "P":
                    self.send("y", s, name)
                if name == "D":
                    self.send(1, s, name)
                    self.send(-1, s, name)
                self.send("core", s, name)
            self.when(cond, go)

    def far(self, k, column):
        for dz, cond, sign in self.step(k):
            def go(dz=dz, sign=sign):
                s = self.shard(dz, column)
                self.wait(s, "D")
                if k < 3:
                    self.along(dz, sign, s, "D")
                self.send("core", s, "D")
            self.when(cond, go)

    def from_y(self, k, column, name):
        for dz, cond, sign in self.step(k):
            def go(dz=dz):
                s = self.shard(dz, column)
                self.wait(s, name)
                self.send("core", s, name)
            self.when(cond, go)

    def sibling(self, k, column):
        for dz, cond, sign in self.step(k):
            def go(dz=dz):
                s = self.shard(dz, column)
                self.await_rows(self.place(1 - self.c, s, 0, MAIN, 0), self.bsem.at[s], False)
            self.when(cond, go)

    def await_rows(self, ref, sem, sent):
        desc = pltpu.make_async_remote_copy(
            src_ref=ref, dst_ref=ref, send_sem=sem, recv_sem=sem, device_id=self.dev["core"], device_id_type=MESH_ID
        )
        if sent:
            desc.wait_send()
        else:
            desc.wait_recv()

    def sibling_far(self, near):
        half = self.z // 2 if near else 1 - self.z // 2
        rows = (DEPTH - 1 if near else DEPTH) * FAR
        self.await_rows(self.w.at[1 - self.c, pl.ds(0, rows)], self.bsem.at[self.shards + half], False)
        return half

    def greet(self):
        bar = pltpu.get_barrier_semaphore()
        for to in LINKS:
            def hello(to=to):
                pl.semaphore_signal(bar, inc=1, device_id=self.dev[to], device_id_type=MESH_ID)
            self.when(self.can[to], hello)

    def meet(self):
        near = 3 + (self.z > 0).astype(jnp.int32) + (self.z < DEPTH - 1).astype(jnp.int32)
        pl.semaphore_wait(pltpu.get_barrier_semaphore(), near)

    def finish(self):
        handed = self.handed()
        plane = MAIN - handed
        for i, to in enumerate(LINKS):
            if to in (1, -1):
                for z in range(DEPTH):
                    depth = (z + 1 if to == 1 else DEPTH - z) * (plane + 2 * FAR)
                    if 0 <= z + to < DEPTH:
                        def done(depth=depth, i=i):
                            self.await_rows(self.w.at[0, pl.ds(0, depth)], self.ssem.at[i], True)
                        pl.when(self.z == z)(done)
            else:
                rows = {"x": DEPTH * plane + FAR, "y": (self.shards - 1) * handed, "core": (self.shards - 1) * (MAIN + FAR)}[to]
                self.await_rows(self.w.at[0, pl.ds(0, rows)], self.ssem.at[i], True)

    def local(self, fin, fout, sem):
        s = self.shard(0, 0)
        out = []
        for m, src in enumerate((fin, fout)):
            out.append(pltpu.make_async_copy(src.at[pl.ds(0, MAIN)], self.place(m, s, 0, MAIN, 0), sem.at[2 * m]))
            out.append(pltpu.make_async_copy(src.at[pl.ds(MAIN, FAR)], self.place(m, s, MAIN, FAR, DD), sem.at[2 * m + 1]))
        for c in out:
            c.start()
        return out


def run_events(g, toks):
    for ev in toks:
        kind, k, name = ev[0], ev[1], ev[2:]
        if kind == "s":
            for to in ("x",) if k == "x" else (1, -1):
                g.send(to, g.shard(0, 0), ev[3:])
        elif kind == "z":
            g.from_z(int(k), name)
        elif kind == "x":
            g.from_x(int(k), name)
        elif kind in "de":
            g.far(int(k), int(kind == "e"))
        elif kind in "Yy":
            g.from_y(int(k), int(kind == "y"), name)


ORDER = (
    "sx:P1", "sz:P1", "sx:A0", "sz:P0", "sx:A1", "x0P1", "sx:P0", "sx:D", "CM", "z1P1", "sz:A1", "z1P0", "CQ0", "sz:D", "x0P0", "x0A1", "z2P0", "sz:A0", "y0O1",
    "z2P1", "CQ1", "x0D", "CQ2", "x1P1", "z3P0", "CQ3", "z1A1", "z3P1", "x0A0", "e1", "z1A0", "Y1O0", "x3P0", "z2A1", "y0O0", "x1P0", "CA0", "CA1", "CA2", "Y2O1", "x2P1",
    "Y3O0", "CA3", "CL", "y3O0", "Y1O1", "d1", "x2P0", "z2A0", "F0", "y1O1", "x1A1", "y1O0", "x1A0", "z3A1", "e2", "Y2O0", "d2", "F1", "x2A0", "x2A1", "x3P1", "Y3O1",
    "z3A0", "y2O1", "y2O0", "x3A1", "F2", "x3A0", "y3O1", "d3", "e3", "F3", "G0", "G1",
)


class Reduce:
    def __init__(self, g, part, got, along, total, ssem, rsem):
        self.g, self.part, self.got, self.along, self.total, self.ssem, self.rsem = g, part, got, along, total, ssem, rsem
        y, x, z, c = g.y, g.x, g.z, g.c
        self.mine = (y * 2 + x) * 2 + c
        spots = [
            (yy, xx, cc) for cc in (1 - c, c) for yy, xx in ((1 - y, 1 - x), (1 - y, x), (y, 1 - x), (y, x))
        ][:7]
        self.mates = [((yy * 2 + xx) * 2 + cc, (yy * 2 + cc, z * 2 + xx)) for yy, xx, cc in spots]
        self.far_z = [(lax.rem(z + i, DEPTH), (y * 2 + c, lax.rem(z + i, DEPTH) * 2 + x)) for i in range(1, DEPTH)]

    def copy(self, src, dst, stage, recv, dev):
        return pltpu.make_async_remote_copy(
            src_ref=src, dst_ref=dst, send_sem=self.ssem.at[stage], recv_sem=self.rsem.at[stage, recv], device_id=dev,
            device_id_type=MESH_ID,
        )

    def scatter(self):
        for owner, dev in self.mates:
            self.copy(self.part.at[owner], self.got.at[self.mine], 0, self.mine, dev).start()

    def along_z(self):
        for owner, dev in self.mates:
            self.copy(self.part.at[owner], self.got.at[owner], 0, owner, dev).wait_recv()
        self.got[self.mine] = self.part[self.mine]
        parts = [self.got[i].astype(F32) for i in range(8)]
        z = self.g.z
        self.along[z] = (
            ((parts[0] + parts[1]) + (parts[2] + parts[3])) + ((parts[4] + parts[5]) + (parts[6] + parts[7]))
        ).astype(BF16)
        for zz, dev in self.far_z:
            self.copy(self.along.at[z], self.along.at[z], 1, z, dev).start()

    def spread(self):
        for zz, dev in self.far_z:
            self.copy(self.along.at[zz], self.along.at[zz], 1, zz, dev).wait_recv()
        rows = [self.along[i].astype(F32) for i in range(DEPTH)]
        self.total[self.mine] = ((rows[0] + rows[1]) + (rows[2] + rows[3])).astype(BF16)
        for owner, dev in self.mates:
            self.copy(self.total.at[self.mine], self.total.at[self.mine], 2, self.mine, dev).start()

    def collect(self, dpk_ref, dpv_ref):
        for owner, dev in self.mates:
            self.copy(self.total.at[owner], self.total.at[owner], 2, owner, dev).wait_recv()
        for i in range(8):
            both = self.total[i].astype(F32)
            dpk_ref[:, i * 128:(i + 1) * 128] = both[:PREF]
            dpv_ref[:, i * 128:(i + 1) * 128] = both[HELD:HELD + PREF]

    def finish(self):
        for stage, n in enumerate((7, DEPTH - 1, 7)):
            ref = self.got.at[pl.ds(0, n)]
            self.copy(ref, ref, stage, 0, self.g.dev["core"]).wait_send()


def kernel(
    remote,
    x_hbm, seg_hbm, wq_hbm, wk_hbm, wv_hbm, wo_hbm, g1_hbm, b1_hbm, fin_hbm, fout_hbm, g2_hbm, b2_hbm, pk_hbm, pv_hbm, cot_hbm,
    out_hbm, gin_hbm, dpk_ref, dpv_ref,
    x, cot, wq, wk, wv, wo, w, q, k, v, km, qm, vm, prob, prob_t, ppref, ppref_t, mixed, mixed_low, n1, rstd1, hidden, hid_low,
    dgelu, gp, acc, gr2, glow, bias, live, pad_k, pad_v, ds, ds_t, outv, dq, dk, dv, sem_in, sem_w, sem_out,
    seg_ref, g1, b1, g2, b2, pk_ref, pv_ref,
    part, *comm,
):
    slots, width = x.shape
    units = w.shape[1]
    nq = width // LANES
    srcs = [(x_hbm, x), (wq_hbm, wq), (wk_hbm, wk), (wv_hbm, wv), (wo_hbm, wo), (cot_hbm, cot)]
    srcs += [(seg_hbm, seg_ref), (pk_hbm, pk_ref), (pv_hbm, pv_ref), (g1_hbm, g1), (b1_hbm, b1), (g2_hbm, g2), (b2_hbm, b2)]
    loads = [pltpu.make_async_copy(s, d, sem_in.at[i]) for i, (s, d) in enumerate(srcs)]
    if remote:
        ssem, rsem, bsem, got, along, total, red_s, red_r = comm
        g = Gather(w, units // (MAIN + FAR), ssem, rsem, bsem)
        red = Reduce(g, part, got, along, total, red_s, red_r)
        g.greet()
        wloads = g.local(fin_hbm, fout_hbm, sem_w)
    else:
        wloads = [pltpu.make_async_copy(src, w.at[m], sem_w.at[m]) for m, src in enumerate((fin_hbm, fout_hbm))]
    if not remote:
        for c in loads + wloads:
            c.start()
    bd_shape = (QUAD * PAD, LANES)
    block_diag = lax.broadcasted_iota(jnp.int32, bd_shape, 0) // PAD == lax.broadcasted_iota(jnp.int32, bd_shape, 1) // 64
    lane = lax.broadcasted_iota(jnp.int32, (1, QUAD * PAD), 1)

    def cols_of(j):
        return slice(j * LANES, (j + 1) * LANES)

    def pref_bias(h):
        return jnp.where((lane // PAD == h) & (lane % PAD < PREF), 0.0, NEG)

    def block(ref, j):
        part = ref[:, cols_of(j)]
        return jnp.where(block_diag, jnp.concatenate([part] * QUAD, axis=0), 0.0).astype(BF16)

    def masks():
        for c in loads[6:9]:
            c.wait()
        seg_row = jnp.broadcast_to(seg_ref[...].astype(F32), (slots, slots))
        seg_col = seg_row.T
        bias[...] = jnp.where((seg_row == seg_col) & (seg_row < PAIRS), 0.0, NEG)
        live[...] = (seg_col[:, :128] < PAIRS).astype(F32)
        pad_k[...] = jnp.zeros_like(pad_k)
        pad_v[...] = jnp.zeros_like(pad_v)
        pad_k[0:PREF, :] = pk_ref[...]
        pad_v[0:PREF, :] = pv_ref[...]

    def project(j):
        cols = cols_of(j)
        if j == 0:
            for i in range(4):
                loads[i].wait()
        q[:, cols] = (nn(x[...], wq[:, cols]) * 0.125).astype(BF16)
        k[:, cols] = nn(x[...], wk[:, cols]).astype(BF16)
        v[:, cols] = nn(x[...], wv[:, cols]).astype(BF16)
        for h in range(QUAD):
            rows = slice(h * slots, (h + 1) * slots)
            keep = head_mask((slots, LANES), h)
            qm[j, rows, :] = jnp.where(keep, q[:, cols], jnp.zeros((), BF16))
            km[j, rows, :] = jnp.where(keep, k[:, cols], jnp.zeros((), BF16))
            vm[j, rows, :] = jnp.where(keep, v[:, cols], jnp.zeros((), BF16))
        km[j, QUAD * slots:, :] = block(pad_k, j)
        vm[j, QUAD * slots:, :] = block(pad_v, j)

    def attend(j):
        cols = cols_of(j)
        sp_all = nt(q[:, cols], km[j, QUAD * slots:, :])
        pp_all = jnp.zeros((slots, QUAD * PAD), F32)
        for h in range(QUAD):
            rows = slice(h * slots, (h + 1) * slots)
            s = nt(q[:, cols], km[j, rows, :]) + bias[...]
            sp = sp_all + pref_bias(h)
            top = jnp.maximum(jnp.max(s, axis=-1, keepdims=True), jnp.max(sp, axis=-1, keepdims=True))
            e = jnp.exp(s - top)
            ep = jnp.exp(sp - top)
            inv = 1.0 / (jnp.sum(e, axis=-1, keepdims=True) + jnp.sum(ep, axis=-1, keepdims=True))
            p = e * inv
            prob[j * QUAD + h] = p
            ds[:, rows] = p.astype(BF16)
            prob_t[j, :, rows] = p.T.astype(BF16)
            pp_all = pp_all + ep * inv
        ppref[j] = pp_all
        ppref_t[j] = pp_all.T
        ds[:, QUAD * slots:] = pp_all.astype(BF16)
        o = nn(ds[...], vm[j])
        mixed[:, cols] = o
        mixed_low[:, cols] = o.astype(BF16)

    def norm1():
        for c in (loads[4], loads[9], loads[10]):
            c.wait()
        for j in range(nq):
            acc[:, cols_of(j)] = nn(mixed_low[...], wo[:, cols_of(j)])

        def rows_of(i, carry):
            r = pl.ds(pl.multiple_of(i * ROWB, ROWB), ROWB)
            n, rstd = normalize(x[r, :].astype(F32) + acc[r, :])
            n1[r, :] = n
            rstd1[r, :] = jnp.broadcast_to(rstd, (ROWB, 128))
            h = n * g1[...] + b1[...]
            hidden[r, :] = h
            hid_low[r, :] = h.astype(BF16)
            acc[r, :] = jnp.zeros((ROWB, width), F32)
            return carry

        lax.fori_loop(0, slots // ROWB, rows_of, 0, unroll=UNROLL)

    def feed(base, sizes):
        at, total = 0, sum(sizes)
        for n in sizes:
            act, slope = gelu_parts(nt(hid_low[...], w[0, pl.ds(base + at, n), :]))
            dgelu[:, pl.ds(base + at, n)] = slope
            gp[:, at:at + n] = act.astype(BF16)
            at += n
        for j in range(nq):
            acc[:, cols_of(j)] += nn(gp[:, :total], w[1, pl.ds(base, total), cols_of(j)])

    if remote:
        g.meet()
        for c in wloads:
            c.wait()
        pair = 2 * MAIN
        events = []
        for tok in ORDER:
            if tok[0] not in "CFG":
                events.append(tok)
                continue
            if events:
                run_events(g, events)
                events = []
            if tok == "CM":
                for c in loads[6:9] + loads[:6] + loads[9:]:
                    c.start()
                masks()
            elif tok == "CL":
                norm1()
            elif tok[:2] == "CQ":
                project(int(tok[2]))
            elif tok[:2] == "CA":
                attend(int(tok[2]))
            elif tok[0] == "F":
                dist = int(tok[1])
                if dist:
                    g.sibling(dist, 0)
                g.sibling(dist, 1)
                for dz, cond, sign in g.step(dist):
                    def go(dz=dz):
                        where = jnp.clip(g.z + dz, 0, DEPTH - 1)
                        feed(pl.multiple_of(where * pair, 128), (256, 256, 256, 128))
                    g.when(cond, go)
            else:
                half = g.sibling_far(tok == "G0")
                feed(pl.multiple_of(units - 2 * LANES + half * LANES, LANES), (LANES,))

    else:
        masks()
        for j in range(nq):
            project(j)
        for j in range(nq):
            attend(j)
        norm1()
        for c in wloads:
            c.wait()

        def feed_step(s, carry):
            feed(pl.multiple_of(s * 2 * LANES, 2 * LANES), (256, 256))
            return carry

        lax.fori_loop(0, units // (2 * LANES), feed_step, 0)

    for c in (loads[5], loads[11], loads[12]):
        c.wait()

    def norm2_rows(i, carry):
        r = pl.ds(pl.multiple_of(i * ROWB, ROWB), ROWB)
        n, rstd = normalize(hidden[r, :] + acc[r, :])
        (out_hbm if remote else outv)[r, :] = (n * g2[...] + b2[...]).astype(BF16)
        dn = cot[r, :].astype(F32) * live[r, 0:1] * g2[...]
        grad = norm_back(dn, n, rstd)
        gr2[r, :] = grad
        glow[r, :] = grad.astype(BF16)
        return carry

    lax.fori_loop(0, slots // ROWB, norm2_rows, 0, unroll=UNROLL)
    if not remote:
        out_copy = pltpu.make_async_copy(outv, out_hbm, sem_out.at[0])
        out_copy.start()

    for u in range(units // LANES):
        rows = slice(u * LANES, (u + 1) * LANES)
        gp[:, rows] = (nt(glow[...], w[1, rows, :]) * dgelu[:, rows]).astype(BF16)
    for j in range(nq):
        acc[:, cols_of(j)] = gr2[:, cols_of(j)] + nn(gp[...], w[0, :, cols_of(j)])

    def norm1_back(i, carry):
        r = pl.ds(pl.multiple_of(i * ROWB, ROWB), ROWB)
        grad = norm_back(acc[r, :] * g1[...], n1[r, :], rstd1[r, 0:1])
        gr2[r, :] = grad
        glow[r, :] = grad.astype(BF16)
        return carry

    lax.fori_loop(0, slots // ROWB, norm1_back, 0, unroll=UNROLL)

    for j in range(nq):
        hid_low[:, cols_of(j)] = nt(glow[...], wo[cols_of(j), :]).astype(BF16)
    ones_shape = (LANES, QUAD * PAD)
    ones = (lax.broadcasted_iota(jnp.int32, ones_shape, 0) // 64 == lax.broadcasted_iota(jnp.int32, ones_shape, 1) // PAD).astype(BF16)
    ones_t = block_diag.astype(BF16)
    delta_t, halves = [], []
    for j in range(nq):
        cols = cols_of(j)
        do = hid_low[:, cols]
        prod = do.astype(F32) * mixed[:, cols]
        high = prod.astype(BF16)
        halves.append((high, (prod - high.astype(F32)).astype(BF16)))
        delta_t.append(nt(ones_t, halves[j][0]) + nt(ones_t, halves[j][1]))
        dsp_t = (ppref_t[j] * (nt(vm[j, QUAD * slots:, :], do) - delta_t[j])).astype(BF16)
        gk = jnp.where(block_diag, nn(dsp_t, q[:, cols]), 0.0)
        gv = jnp.where(block_diag, nn(ppref_t[j].astype(BF16), do), 0.0)
        both = jnp.concatenate([sum(t[i * PAD:i * PAD + HELD] for i in range(QUAD)) for t in (gk, gv)], axis=0)
        for i in range(2):
            part[2 * j + i] = both[:, i * 128:(i + 1) * 128].astype(part.dtype)
    if remote:
        red.scatter()
    for j in range(nq):
        cols = cols_of(j)
        do = hid_low[:, cols]
        delta = nn(halves[j][0], ones) + nn(halves[j][1], ones)
        ds[:, QUAD * slots:] = (ppref[j] * (nt(do, vm[j, QUAD * slots:, :]) - delta)).astype(BF16)
        for h in range(QUAD):
            rows = slice(h * slots, (h + 1) * slots)
            vh = vm[j, rows, :]
            ds[:, rows] = (prob[j * QUAD + h] * (nt(do, vh) - delta[:, h * PAD:h * PAD + 1])).astype(BF16)
            ds_t[:, rows] = (prob_t[j, :, rows].astype(F32) * (nt(vh, do) - delta_t[j][h * PAD:h * PAD + 1, :])).astype(BF16)
        dq[:, cols] = nn(ds[...], km[j]).astype(BF16) * jnp.asarray(0.125, BF16)
        dk[:, cols] = nn(ds_t[...], qm[j]).astype(BF16)
        dom = jnp.concatenate([jnp.where(head_mask((slots, LANES), h), do, jnp.zeros((), BF16)) for h in range(QUAD)], axis=0)
        dv[:, cols] = nn(prob_t[j], dom).astype(BF16)
        if remote and j == 0:
            g.finish()
        if remote and j == 2:
            red.along_z()

    if not remote:
        out_copy.wait()
    for j in range(nq):
        cols = cols_of(j)
        grad = gr2[:, cols] + nt(dq[...], wq[cols, :]) + nt(dk[...], wk[cols, :]) + nt(dv[...], wv[cols, :])
        (gin_hbm if remote else outv)[:, cols] = grad.astype(BF16)
    if remote:
        red.spread()
        red.collect(dpk_ref, dpv_ref)
        red.finish()
    else:
        for i in range(8):
            dpk_ref[:, i * 128:(i + 1) * 128] = part[i, :PREF]
            dpv_ref[:, i * 128:(i + 1) * 128] = part[i, HELD:HELD + PREF]
        done = pltpu.make_async_copy(outv, gin_hbm, sem_out.at[1])
        done.start()
        done.wait()


def settle(*refs):
    half = len(refs) // 2
    copies = [pltpu.make_async_copy(refs[i], refs[half + i], refs[-1].at[i]) for i in range(half)]
    for c in copies:
        c.start()
    for c in copies:
        c.wait()


def body(
    remote, inputs, seg_ids, w_query, w_key, w_value, w_attn_out, norm1_gain, norm1_bias, ffn_in, ffn_out, norm2_gain,
    norm2_bias, prefix_key, prefix_value, cotangent,
):
    rows, slots, width = inputs.shape
    if remote:
        fin, fout = ffn_in, ffn_out
        units = ffn_in.shape[0] * lax.axis_size("ffn")
    else:
        fin = lax.all_gather(ffn_in, "ffn", axis=0, tiled=True)
        fout = lax.all_gather(ffn_out, "ffn", axis=0, tiled=True)
        units = fin.shape[0]
    nq = width // LANES
    any_spec = pl.BlockSpec(memory_space=pl.ANY)
    vmem = pl.BlockSpec(memory_space=pltpu.VMEM)

    def run(x, seg, cot):
        def sq(n=1):
            return pltpu.VMEM((slots, n * width), BF16)

        full = pltpu.VMEM((slots, width), F32)
        wide = QUAD * slots + QUAD * PAD
        scratch = [
            sq(), sq(),
            *[pltpu.VMEM((width, width), BF16) for _ in range(4)],
            pltpu.VMEM((2, units, width), BF16),
            sq(), sq(), sq(),
            pltpu.VMEM((nq, wide, LANES), BF16),
            pltpu.VMEM((nq, QUAD * slots, LANES), BF16),
            pltpu.VMEM((nq, wide, LANES), BF16),
            pltpu.VMEM((HEADS, slots, slots), F32),
            pltpu.VMEM((nq, slots, QUAD * slots), BF16),
            pltpu.VMEM((nq, slots, QUAD * PAD), F32),
            pltpu.VMEM((nq, QUAD * PAD, slots), F32),
            full, sq(),
            full, pltpu.VMEM((slots, 128), F32), full, sq(),
            pltpu.VMEM((slots, units), F32),
            pltpu.VMEM((slots, units), BF16),
            full, full, sq(),
            pltpu.VMEM((slots, slots), F32),
            pltpu.VMEM((slots, 128), F32),
            pltpu.VMEM((PAD, width), F32), pltpu.VMEM((PAD, width), F32),
            pltpu.VMEM((slots, wide), BF16),
            pltpu.VMEM((slots, QUAD * slots), BF16),
            sq(), sq(), sq(), sq(),
            pltpu.SemaphoreType.DMA((13,)),
            pltpu.SemaphoreType.DMA((4,)),
            pltpu.SemaphoreType.DMA((2,)),
            pltpu.VMEM((1, slots), jnp.int32),
            *[pltpu.VMEM((1, width), F32) for _ in range(4)],
            *[pltpu.VMEM((PREF, width), F32) for _ in range(2)],
            pltpu.VMEM((8, 2 * HELD, 128), BF16 if remote else F32),
        ]
        if remote:
            shards = lax.axis_size("ffn")
            scratch += [
                pltpu.SemaphoreType.DMA((len(LINKS),)),
                pltpu.SemaphoreType.DMA((shards, 7)),
                pltpu.SemaphoreType.DMA((shards + 2,)),
                pltpu.VMEM((8, 2 * HELD, 128), BF16),
                pltpu.VMEM((DEPTH, 2 * HELD, 128), BF16),
                pltpu.VMEM((8, 2 * HELD, 128), BF16),
                pltpu.SemaphoreType.DMA((3,)),
                pltpu.SemaphoreType.DMA((3, 8)),
            ]
        outs = (((slots, width), BF16), ((slots, width), BF16), ((PREF, width), F32), ((PREF, width), F32))
        params = {"collective_id": 0, "has_side_effects": True} if remote else {}
        return pl.pallas_call(
            functools.partial(kernel, remote),
            out_shape=tuple((pltpu.VMEM if remote else jax.ShapeDtypeStruct)(*t) for t in outs),
            in_specs=[any_spec] * 15,
            out_specs=(vmem,) * 4 if remote else (any_spec, any_spec, vmem, vmem),
            scratch_shapes=scratch,
            compiler_params=pltpu.CompilerParams(vmem_limit_bytes=60 * 2**20, **params),
        )(x, seg, w_query, w_key, w_value, w_attn_out, norm1_gain.reshape(1, width), norm1_bias.reshape(1, width),
          fin, fout, norm2_gain.reshape(1, width), norm2_bias.reshape(1, width), prefix_key, prefix_value, cot)

    if remote and rows == 1:
        made = [jnp.expand_dims(t, 0) if i < 2 else t for i, t in enumerate(run(inputs[0], seg_ids, cotangent[0]))]
        return pl.pallas_call(
            settle,
            out_shape=[jax.ShapeDtypeStruct(t.shape, t.dtype) for t in made],
            in_specs=[vmem] * 4,
            out_specs=[any_spec] * 4,
            scratch_shapes=[pltpu.SemaphoreType.DMA((4,))],
            compiler_params=pltpu.CompilerParams(vmem_limit_bytes=2**20),
        )(*made)
    parts = [run(inputs[r], seg_ids[r:r + 1], cotangent[r]) for r in range(rows)]
    out = jnp.stack([p[0] for p in parts])
    gin = jnp.stack([p[1] for p in parts])
    dpk, dpv = parts[0][2:]
    if not remote:
        dpk, dpv = lax.psum((sum(p[2] for p in parts), sum(p[3] for p in parts)), ("dp", "ffn"))
    return out, gin, dpk, dpv


def solution(mesh):
    row = P(("dp", "ffn"), None, None)
    remote = mesh.shape["ffn"] == 2 * DEPTH and mesh.shape["dp"] == 4
    return jax.shard_map(
        functools.partial(body, remote),
        mesh=mesh,
        in_specs=(row, P(("dp", "ffn"), None), P(), P(), P(), P(), P(), P(), P("ffn", None), P("ffn", None), P(), P(),
                  P(), P(), row),
        out_specs=(row, row, P(), P()),
        check_vma=False,
    )
```

```python
import functools

import jax
import jax.numpy as jnp
from jax import lax
from jax.experimental import pallas as pl
from jax.experimental.pallas import tpu as pltpu
from jax.sharding import PartitionSpec as P

HEADS = 16
PREF = 20
PAIRS = 7
EPS = 1e-05
NEG = -1e30
QUAD = 4
LANES = 256
PAD = 32
HELD = 24
ROWB = 16
UNROLL = 16
F32 = jnp.float32
BF16 = jnp.bfloat16


def nt(a, b):
    return lax.dot_general(a, b, (((1,), (1,)), ((), ())), preferred_element_type=F32)


def nn(a, b):
    return lax.dot_general(a, b, (((1,), (0,)), ((), ())), preferred_element_type=F32)


def head_mask(shape, h):
    return lax.broadcasted_iota(jnp.int32, shape, 1) // 64 == h


def normalize(r):
    center = r - jnp.mean(r, axis=-1, keepdims=True)
    spread = jnp.mean(center * center, axis=-1, keepdims=True)
    rstd = lax.rsqrt(spread + EPS)
    return center * rstd, rstd


def norm_back(dn, n, rstd):
    return rstd * (dn - jnp.mean(dn, axis=-1, keepdims=True) - n * jnp.mean(dn * n, axis=-1, keepdims=True))


def gelu_parts(pre):
    cdf = 0.5 * (1.0 + lax.erf(pre * 0.7071067811865476))
    return pre * cdf, cdf + pre * (0.3989422804014327 * jnp.exp(-0.5 * pre * pre))


MESH_ID = pl.DeviceIdType.MESH
DEPTH = 4
LINKS = ("x", "y", "core", 1, -1)
PARTS = {"A0": 64, "A1": 64, "P0": 80, "P1": 80}
MAIN = 448
FAR = 64
A0, A1, B0, B1, C0, C1, DD = range(7)


class Gather:
    def __init__(self, w, shards, ssem, rsem, bsem):
        self.w, self.shards, self.ssem, self.rsem, self.bsem = w, shards, ssem, rsem, bsem
        d, f = lax.axis_index("dp"), lax.axis_index("ffn")
        self.y, self.c = d // 2, lax.rem(d, 2)
        self.z, self.x = f // 2, lax.rem(f, 2)
        self.dev = {
            "core": (self.y * 2 + 1 - self.c, f),
            "y": ((1 - self.y) * 2 + self.c, f),
            "x": (d, self.z * 2 + 1 - self.x),
            1: (d, jnp.minimum(self.z + 1, DEPTH - 1) * 2 + self.x),
            -1: (d, jnp.maximum(self.z - 1, 0) * 2 + self.x),
        }
        self.can = {1: lambda: self.z < DEPTH - 1, -1: lambda: self.z > 0, "x": None, "y": None, "core": None}

    def part(self, name):
        rows = PARTS
        if name == "D":
            return MAIN, FAR, DD
        if name[0] == "A":
            return rows["A0"] * int(name[1]), rows[name], int(name[1])
        plane = self.y if name[0] == "P" else 1 - self.y
        i = int(name[1])
        off = rows["A0"] + rows["A1"] + rows["P0"] * i + plane * self.handed()
        return pl.multiple_of(off, 16), rows["P%d" % i], B0 + i + 2 * plane

    def handed(self):
        return PARTS["P0"] + PARTS["P1"]

    def place(self, m, s, off, rows, num):
        if isinstance(num, int) and num == DD:
            start = self.shards * MAIN + s * FAR
        else:
            start = s * MAIN + off
        return self.w.at[m, pl.ds(pl.multiple_of(start, 16), rows)]

    def copy(self, to, s, part):
        off, rows, num = part
        ref = self.place(self.c, s, off, rows, num)
        if to == "core":
            far = isinstance(num, int) and num == DD
            recv = self.bsem.at[self.shards + s // DEPTH if far else s]
        else:
            recv = self.rsem.at[s, num]
        return pltpu.make_async_remote_copy(
            src_ref=ref, dst_ref=ref, send_sem=self.ssem.at[LINKS.index(to)], recv_sem=recv, device_id=self.dev[to],
            device_id_type=MESH_ID,
        )

    def start(self, to, s, name):
        self.copy(to, s, self.part(name)).start()

    def send(self, to, s, name):
        desc = self.copy(to, s, self.part(name))
        can = self.can[to]
        if can is None:
            desc.start()
        else:
            pl.when(can())(desc.start)

    def when(self, cond, fn):
        if cond is None:
            fn()
        else:
            pl.when(cond())(fn)

    def shard(self, dz, column):
        return jnp.clip(self.z + dz, 0, DEPTH - 1) * 2 + (self.x if column == 0 else 1 - self.x)

    def wait(self, s, name):
        self.copy("x", s, self.part(name)).wait_recv()

    def step(self, k):
        if k == 0:
            return [(0, None, 0)]
        if k == 1:
            return [(1, self.can[1], 1), (-1, self.can[-1], -1)]
        dz = jnp.where(self.z < DEPTH // 2, k, -k)
        if k == 2:
            return [(dz, None, None)]
        return [(dz, lambda: jnp.logical_or(self.z == 0, self.z == DEPTH - 1), None)]

    def along(self, dz, sign, s, name):
        if sign is None:
            pl.when(self.z == 1)(lambda: self.start(-1, s, name))
            pl.when(self.z == DEPTH - 2)(lambda: self.start(1, s, name))
        elif sign:
            self.send(-sign, s, name)

    def from_z(self, k, name):
        for dz, cond, sign in self.step(k):
            def go(dz=dz, sign=sign):
                s = self.shard(dz, 0)
                self.wait(s, name)
                if k < 3:
                    self.along(dz, sign, s, name)
                if name[0] == "P":
                    self.send("y", s, name)
                self.send("x", s, name)
                self.send("core", s, name)
            self.when(cond, go)

    def from_x(self, k, name):
        for dz, cond, sign in self.step(k):
            def go(dz=dz):
                s = self.shard(dz, 1)
                self.wait(s, name)
                if name[0] == "P":
                    self.send("y", s, name)
                if name == "D":
                    self.send(1, s, name)
                    self.send(-1, s, name)
                self.send("core", s, name)
            self.when(cond, go)

    def far(self, k, column):
        for dz, cond, sign in self.step(k):
            def go(dz=dz, sign=sign):
                s = self.shard(dz, column)
                self.wait(s, "D")
                if k < 3:
                    self.along(dz, sign, s, "D")
                self.send("core", s, "D")
            self.when(cond, go)

    def from_y(self, k, column, name):
        for dz, cond, sign in self.step(k):
            def go(dz=dz):
                s = self.shard(dz, column)
                self.wait(s, name)
                self.send("core", s, name)
            self.when(cond, go)

    def sibling(self, k, column):
        for dz, cond, sign in self.step(k):
            def go(dz=dz):
                s = self.shard(dz, column)
                self.await_rows(self.place(1 - self.c, s, 0, MAIN, 0), self.bsem.at[s], False)
            self.when(cond, go)

    def await_rows(self, ref, sem, sent):
        desc = pltpu.make_async_remote_copy(
            src_ref=ref, dst_ref=ref, send_sem=sem, recv_sem=sem, device_id=self.dev["core"], device_id_type=MESH_ID
        )
        if sent:
            desc.wait_send()
        else:
            desc.wait_recv()

    def sibling_far(self, near):
        half = self.z // 2 if near else 1 - self.z // 2
        rows = (DEPTH - 1 if near else DEPTH) * FAR
        self.await_rows(self.w.at[1 - self.c, pl.ds(0, rows)], self.bsem.at[self.shards + half], False)
        return half

    def greet(self):
        bar = pltpu.get_barrier_semaphore()
        for to in LINKS:
            def hello(to=to):
                pl.semaphore_signal(bar, inc=1, device_id=self.dev[to], device_id_type=MESH_ID)
            self.when(self.can[to], hello)

    def meet(self):
        near = 3 + (self.z > 0).astype(jnp.int32) + (self.z < DEPTH - 1).astype(jnp.int32)
        pl.semaphore_wait(pltpu.get_barrier_semaphore(), near)

    def finish(self):
        handed = self.handed()
        plane = MAIN - handed
        for i, to in enumerate(LINKS):
            if to in (1, -1):
                for z in range(DEPTH):
                    depth = (z + 1 if to == 1 else DEPTH - z) * (plane + 2 * FAR)
                    if 0 <= z + to < DEPTH:
                        def done(depth=depth, i=i):
                            self.await_rows(self.w.at[0, pl.ds(0, depth)], self.ssem.at[i], True)
                        pl.when(self.z == z)(done)
            else:
                rows = {"x": DEPTH * plane + FAR, "y": (self.shards - 1) * handed, "core": (self.shards - 1) * (MAIN + FAR)}[to]
                self.await_rows(self.w.at[0, pl.ds(0, rows)], self.ssem.at[i], True)

    def local(self, fin, fout, sem):
        s = self.shard(0, 0)
        out = []
        for m, src in enumerate((fin, fout)):
            out.append(pltpu.make_async_copy(src.at[pl.ds(0, MAIN)], self.place(m, s, 0, MAIN, 0), sem.at[2 * m]))
            out.append(pltpu.make_async_copy(src.at[pl.ds(MAIN, FAR)], self.place(m, s, MAIN, FAR, DD), sem.at[2 * m + 1]))
        for c in out:
            c.start()
        return out


def run_events(g, toks):
    for ev in toks:
        kind, k, name = ev[0], ev[1], ev[2:]
        if kind == "s":
            for to in ("x",) if k == "x" else (1, -1):
                g.send(to, g.shard(0, 0), ev[3:])
        elif kind == "z":
            g.from_z(int(k), name)
        elif kind == "x":
            g.from_x(int(k), name)
        elif kind in "de":
            g.far(int(k), int(kind == "e"))
        elif kind in "Yy":
            g.from_y(int(k), int(kind == "y"), name)


ORDER = (
    "sx:P1", "sz:P1", "sx:A0", "sx:A1", "sz:P0", "x0P1", "sx:P0", "sx:D", "CM", "z1P1", "sz:A1", "z1P0", "CQ0", "sz:D", "x0P0", "z2P0", "sz:A0", "y0O1", "CQ1",
    "z2P1", "x0D", "CQ2", "x1P1", "z3P0", "CQ3", "z1A1", "z3P1", "e1", "x0A0", "z1A0", "x0A1", "Y1O0", "x3P0", "y0O0", "z2A1", "x1P0", "CA0", "CA1", "CA2", "Y2O1",
    "x2P1", "CA3", "y3O0", "Y1O1", "CL", "Y3O0", "d1", "x2P0", "z2A0", "F0", "y1O1", "x1A1", "y1O0", "x1A0", "z3A1", "e2", "Y2O0", "d2", "F1", "x2A0", "x2A1", "x3P1",
    "Y3O1", "z3A0", "y2O1", "y2O0", "x3A1", "F2", "x3A0", "e3", "y3O1", "d3", "F3", "G0", "G1",
)


class Reduce:
    def __init__(self, g, part, got, along, total, ssem, rsem):
        self.g, self.part, self.got, self.along, self.total, self.ssem, self.rsem = g, part, got, along, total, ssem, rsem
        y, x, z, c = g.y, g.x, g.z, g.c
        flip = lax.rem(z, 2)
        self.mine = (y * 2 + x) * 2 + lax.rem(c + flip, 2)
        spots = [
            (yy, xx, cc) for cc in (c, 1 - c) for yy, xx in ((1 - y, 1 - x), (1 - y, x), (y, 1 - x), (y, x))
        ]
        spots = [spots[i] for i in (0, 4, 1, 2, 5, 6, 7)]
        self.mates = [((yy * 2 + xx) * 2 + lax.rem(cc + flip, 2), (yy * 2 + cc, z * 2 + xx)) for yy, xx, cc in spots]
        self.far_z = [
            (lax.rem(z + i, DEPTH), (y * 2 + lax.rem(c + i, 2), lax.rem(z + i, DEPTH) * 2 + x)) for i in (2, 1, 3)
        ]

    def copy(self, src, dst, stage, recv, dev):
        return pltpu.make_async_remote_copy(
            src_ref=src, dst_ref=dst, send_sem=self.ssem.at[stage], recv_sem=self.rsem.at[stage, recv], device_id=dev,
            device_id_type=MESH_ID,
        )

    def scatter(self):
        for owner, dev in self.mates:
            self.copy(self.part.at[owner], self.got.at[self.mine], 0, self.mine, dev).start()

    def along_z(self):
        for owner, dev in self.mates:
            self.copy(self.part.at[owner], self.got.at[owner], 0, owner, dev).wait_recv()
        self.got[self.mine] = self.part[self.mine]
        parts = [self.got[i].astype(F32) for i in range(8)]
        z = self.g.z
        self.along[z] = (
            ((parts[0] + parts[1]) + (parts[2] + parts[3])) + ((parts[4] + parts[5]) + (parts[6] + parts[7]))
        ).astype(BF16)
        for zz, dev in self.far_z:
            self.copy(self.along.at[z], self.along.at[z], 1, z, dev).start()

    def spread(self):
        for zz, dev in self.far_z:
            self.copy(self.along.at[zz], self.along.at[zz], 1, zz, dev).wait_recv()
        rows = [self.along[i].astype(F32) for i in range(DEPTH)]
        self.total[self.mine] = ((rows[0] + rows[1]) + (rows[2] + rows[3])).astype(BF16)
        for owner, dev in self.mates:
            self.copy(self.total.at[self.mine], self.total.at[self.mine], 2, self.mine, dev).start()

    def collect(self, dpk_ref, dpv_ref):
        for owner, dev in self.mates:
            self.copy(self.total.at[owner], self.total.at[owner], 2, owner, dev).wait_recv()
        for i in range(8):
            both = self.total[i].astype(F32)
            dpk_ref[:, i * 128:(i + 1) * 128] = both[:PREF]
            dpv_ref[:, i * 128:(i + 1) * 128] = both[HELD:HELD + PREF]

    def finish(self):
        for stage, n in enumerate((7, DEPTH - 1, 7)):
            ref = self.got.at[pl.ds(0, n)]
            self.copy(ref, ref, stage, 0, self.g.dev["core"]).wait_send()


def kernel(
    remote,
    x_hbm, seg_hbm, wq_hbm, wk_hbm, wv_hbm, wo_hbm, g1_hbm, b1_hbm, fin_hbm, fout_hbm, g2_hbm, b2_hbm, pk_hbm, pv_hbm, cot_hbm,
    out_hbm, gin_hbm, dpk_ref, dpv_ref,
    x, cot, wq, wk, wv, wo, w, q, k, v, km, qm, vm, prob, prob_t, ppref, ppref_t, mixed, mixed_low, n1, rstd1, hidden, hid_low,
    dgelu, gp, acc, gr2, glow, bias, live, pad_k, pad_v, ds, ds_t, outv, dq, dk, dv, sem_in, sem_w, sem_out,
    seg_ref, g1, b1, g2, b2, pk_ref, pv_ref,
    part, *comm,
):
    slots, width = x.shape
    units = w.shape[1]
    nq = width // LANES
    srcs = [(x_hbm, x), (wq_hbm, wq), (wk_hbm, wk), (wv_hbm, wv), (wo_hbm, wo), (cot_hbm, cot)]
    srcs += [(seg_hbm, seg_ref), (pk_hbm, pk_ref), (pv_hbm, pv_ref), (g1_hbm, g1), (b1_hbm, b1), (g2_hbm, g2), (b2_hbm, b2)]
    loads = [pltpu.make_async_copy(s, d, sem_in.at[i]) for i, (s, d) in enumerate(srcs)]
    if remote:
        ssem, rsem, bsem, got, along, total, red_s, red_r = comm
        g = Gather(w, units // (MAIN + FAR), ssem, rsem, bsem)
        red = Reduce(g, part, got, along, total, red_s, red_r)
        g.greet()
        wloads = g.local(fin_hbm, fout_hbm, sem_w)
    else:
        wloads = [pltpu.make_async_copy(src, w.at[m], sem_w.at[m]) for m, src in enumerate((fin_hbm, fout_hbm))]
    if not remote:
        for c in loads + wloads:
            c.start()
    bd_shape = (QUAD * PAD, LANES)
    block_diag = lax.broadcasted_iota(jnp.int32, bd_shape, 0) // PAD == lax.broadcasted_iota(jnp.int32, bd_shape, 1) // 64
    lane = lax.broadcasted_iota(jnp.int32, (1, QUAD * PAD), 1)

    def cols_of(j):
        return slice(j * LANES, (j + 1) * LANES)

    def pref_bias(h):
        return jnp.where((lane // PAD == h) & (lane % PAD < PREF), 0.0, NEG)

    def block(ref, j):
        part = ref[:, cols_of(j)]
        return jnp.where(block_diag, jnp.concatenate([part] * QUAD, axis=0), 0.0).astype(BF16)

    def masks():
        for c in loads[6:9]:
            c.wait()
        seg_row = jnp.broadcast_to(seg_ref[...].astype(F32), (slots, slots))
        seg_col = seg_row.T
        bias[...] = jnp.where((seg_row == seg_col) & (seg_row < PAIRS), 0.0, NEG)
        live[...] = (seg_col[:, :128] < PAIRS).astype(F32)
        pad_k[...] = jnp.zeros_like(pad_k)
        pad_v[...] = jnp.zeros_like(pad_v)
        pad_k[0:PREF, :] = pk_ref[...]
        pad_v[0:PREF, :] = pv_ref[...]

    def project(j):
        cols = cols_of(j)
        if j == 0:
            for i in range(4):
                loads[i].wait()
        q[:, cols] = (nn(x[...], wq[:, cols]) * 0.125).astype(BF16)
        k[:, cols] = nn(x[...], wk[:, cols]).astype(BF16)
        v[:, cols] = nn(x[...], wv[:, cols]).astype(BF16)
        for h in range(QUAD):
            rows = slice(h * slots, (h + 1) * slots)
            keep = head_mask((slots, LANES), h)
            qm[j, rows, :] = jnp.where(keep, q[:, cols], jnp.zeros((), BF16))
            km[j, rows, :] = jnp.where(keep, k[:, cols], jnp.zeros((), BF16))
            vm[j, rows, :] = jnp.where(keep, v[:, cols], jnp.zeros((), BF16))
        km[j, QUAD * slots:, :] = block(pad_k, j)
        vm[j, QUAD * slots:, :] = block(pad_v, j)

    def attend(j):
        cols = cols_of(j)
        sp_all = nt(q[:, cols], km[j, QUAD * slots:, :])
        pp_all = jnp.zeros((slots, QUAD * PAD), F32)
        for h in range(QUAD):
            rows = slice(h * slots, (h + 1) * slots)
            s = nt(q[:, cols], km[j, rows, :]) + bias[...]
            sp = sp_all + pref_bias(h)
            top = jnp.maximum(jnp.max(s, axis=-1, keepdims=True), jnp.max(sp, axis=-1, keepdims=True))
            e = jnp.exp(s - top)
            ep = jnp.exp(sp - top)
            inv = 1.0 / (jnp.sum(e, axis=-1, keepdims=True) + jnp.sum(ep, axis=-1, keepdims=True))
            p = e * inv
            prob[j * QUAD + h] = p
            ds[:, rows] = p.astype(BF16)
            prob_t[j, :, rows] = p.T.astype(BF16)
            pp_all = pp_all + ep * inv
        ppref[j] = pp_all
        ppref_t[j] = pp_all.T
        ds[:, QUAD * slots:] = pp_all.astype(BF16)
        o = nn(ds[...], vm[j])
        mixed[:, cols] = o
        mixed_low[:, cols] = o.astype(BF16)

    def norm1():
        for c in (loads[4], loads[9], loads[10]):
            c.wait()
        for j in range(nq):
            acc[:, cols_of(j)] = nn(mixed_low[...], wo[:, cols_of(j)])

        def rows_of(i, carry):
            r = pl.ds(pl.multiple_of(i * ROWB, ROWB), ROWB)
            n, rstd = normalize(x[r, :].astype(F32) + acc[r, :])
            n1[r, :] = n
            rstd1[r, :] = jnp.broadcast_to(rstd, (ROWB, 128))
            h = n * g1[...] + b1[...]
            hidden[r, :] = h
            hid_low[r, :] = h.astype(BF16)
            acc[r, :] = jnp.zeros((ROWB, width), F32)
            return carry

        lax.fori_loop(0, slots // ROWB, rows_of, 0, unroll=UNROLL)

    def feed(base, sizes):
        at, total = 0, sum(sizes)
        for n in sizes:
            act, slope = gelu_parts(nt(hid_low[...], w[0, pl.ds(base + at, n), :]))
            dgelu[:, pl.ds(base + at, n)] = slope
            gp[:, at:at + n] = act.astype(BF16)
            at += n
        for j in range(nq):
            acc[:, cols_of(j)] += nn(gp[:, :total], w[1, pl.ds(base, total), cols_of(j)])

    if remote:
        g.meet()
        for c in wloads:
            c.wait()
        pair = 2 * MAIN
        events = []
        for tok in ORDER:
            if tok[0] not in "CFG":
                events.append(tok)
                continue
            if events:
                run_events(g, events)
                events = []
            if tok == "CM":
                for c in loads[6:9] + loads[:6] + loads[9:]:
                    c.start()
                masks()
            elif tok == "CL":
                norm1()
            elif tok[:2] == "CQ":
                project(int(tok[2]))
            elif tok[:2] == "CA":
                attend(int(tok[2]))
            elif tok[0] == "F":
                dist = int(tok[1])
                if dist:
                    g.sibling(dist, 0)
                g.sibling(dist, 1)
                for dz, cond, sign in g.step(dist):
                    def go(dz=dz):
                        where = jnp.clip(g.z + dz, 0, DEPTH - 1)
                        feed(pl.multiple_of(where * pair, 128), (256, 256, 256, 128))
                    g.when(cond, go)
            else:
                half = g.sibling_far(tok == "G0")
                feed(pl.multiple_of(units - 2 * LANES + half * LANES, LANES), (LANES,))

    else:
        masks()
        for j in range(nq):
            project(j)
        for j in range(nq):
            attend(j)
        norm1()
        for c in wloads:
            c.wait()

        def feed_step(s, carry):
            feed(pl.multiple_of(s * 2 * LANES, 2 * LANES), (256, 256))
            return carry

        lax.fori_loop(0, units // (2 * LANES), feed_step, 0)

    for c in (loads[5], loads[11], loads[12]):
        c.wait()

    def norm2_rows(i, carry):
        r = pl.ds(pl.multiple_of(i * ROWB, ROWB), ROWB)
        n, rstd = normalize(hidden[r, :] + acc[r, :])
        (out_hbm if remote else outv)[r, :] = (n * g2[...] + b2[...]).astype(BF16)
        dn = cot[r, :].astype(F32) * live[r, 0:1] * g2[...]
        grad = norm_back(dn, n, rstd)
        gr2[r, :] = grad
        glow[r, :] = grad.astype(BF16)
        return carry

    lax.fori_loop(0, slots // ROWB, norm2_rows, 0, unroll=UNROLL)
    if not remote:
        out_copy = pltpu.make_async_copy(outv, out_hbm, sem_out.at[0])
        out_copy.start()

    for u in range(units // (2 * LANES)):
        rows = slice(u * 2 * LANES, (u + 1) * 2 * LANES)
        gp[:, rows] = (nt(glow[...], w[1, rows, :]) * dgelu[:, rows]).astype(BF16)
    for j in range(nq // 2):
        cols = slice(j * 2 * LANES, (j + 1) * 2 * LANES)
        acc[:, cols] = gr2[:, cols] + nn(gp[...], w[0, :, cols])

    def norm1_back(i, carry):
        r = pl.ds(pl.multiple_of(i * ROWB, ROWB), ROWB)
        grad = norm_back(acc[r, :] * g1[...], n1[r, :], rstd1[r, 0:1])
        gr2[r, :] = grad
        glow[r, :] = grad.astype(BF16)
        return carry

    lax.fori_loop(0, slots // ROWB, norm1_back, 0, unroll=UNROLL)

    for j in range(nq):
        hid_low[:, cols_of(j)] = nt(glow[...], wo[cols_of(j), :]).astype(BF16)
    ones_shape = (LANES, QUAD * PAD)
    ones = (lax.broadcasted_iota(jnp.int32, ones_shape, 0) // 64 == lax.broadcasted_iota(jnp.int32, ones_shape, 1) // PAD).astype(BF16)
    ones_t = block_diag.astype(BF16)
    quads = [hid_low.at[:, cols_of(j)] for j in range(nq)]
    prods = [quads[j][...].astype(F32) * mixed[:, cols_of(j)] for j in range(nq)]
    highs = [t.astype(BF16) for t in prods]
    halves = [(t, (prods[j] - t.astype(F32)).astype(BF16)) for j, t in enumerate(highs)]
    delta_t = [nt(ones_t, a) + nt(ones_t, b) for a, b in halves]
    gv = [nn(ppref_t[j].astype(BF16), quads[j][...]) for j in range(nq)]
    dsp_t = [(ppref_t[j] * (nt(vm[j, QUAD * slots:, :], quads[j][...]) - delta_t[j])).astype(BF16) for j in range(nq)]
    gk = [nn(dsp_t[j], q[:, cols_of(j)]) for j in range(nq)]
    for j in range(nq):
        both = []
        for t in (gk[j], gv[j]):
            t = jnp.where(block_diag, t, 0.0)
            both.append(sum(t[i * PAD:i * PAD + HELD] for i in range(QUAD)))
        both = jnp.concatenate(both, axis=0)
        for i in range(2):
            part[2 * j + i] = both[:, i * 128:(i + 1) * 128].astype(part.dtype)
    if remote:
        red.scatter()
    for j in range(nq):
        cols = cols_of(j)
        do = hid_low[:, cols]
        delta = nn(halves[j][0], ones) + nn(halves[j][1], ones)
        ds[:, QUAD * slots:] = (ppref[j] * (nt(do, vm[j, QUAD * slots:, :]) - delta)).astype(BF16)
        for h in range(QUAD):
            rows = slice(h * slots, (h + 1) * slots)
            vh = vm[j, rows, :]
            ds[:, rows] = (prob[j * QUAD + h] * (nt(do, vh) - delta[:, h * PAD:h * PAD + 1])).astype(BF16)
            ds_t[:, rows] = (prob_t[j, :, rows].astype(F32) * (nt(vh, do) - delta_t[j][h * PAD:h * PAD + 1, :])).astype(BF16)
        dq[:, cols] = nn(ds[...], km[j]).astype(BF16) * jnp.asarray(0.125, BF16)
        dk[:, cols] = nn(ds_t[...], qm[j]).astype(BF16)
        dom = jnp.concatenate([jnp.where(head_mask((slots, LANES), h), do, jnp.zeros((), BF16)) for h in range(QUAD)], axis=0)
        dv[:, cols] = nn(prob_t[j], dom).astype(BF16)
        if remote and j == 0:
            g.finish()
        if remote and j == 2:
            red.along_z()

    if not remote:
        out_copy.wait()
    for j in range(nq):
        cols = cols_of(j)
        grad = gr2[:, cols] + nt(dq[...], wq[cols, :]) + nt(dk[...], wk[cols, :]) + nt(dv[...], wv[cols, :])
        (gin_hbm if remote else outv)[:, cols] = grad.astype(BF16)
    if remote:
        red.spread()
        red.collect(dpk_ref, dpv_ref)
        red.finish()
    else:
        for i in range(8):
            dpk_ref[:, i * 128:(i + 1) * 128] = part[i, :PREF]
            dpv_ref[:, i * 128:(i + 1) * 128] = part[i, HELD:HELD + PREF]
        done = pltpu.make_async_copy(outv, gin_hbm, sem_out.at[1])
        done.start()
        done.wait()


def settle(*refs):
    half = len(refs) // 2
    copies = [pltpu.make_async_copy(refs[i], refs[half + i], refs[-1].at[i]) for i in range(half)]
    for c in copies:
        c.start()
    for c in copies:
        c.wait()


def body(
    remote, inputs, seg_ids, w_query, w_key, w_value, w_attn_out, norm1_gain, norm1_bias, ffn_in, ffn_out, norm2_gain,
    norm2_bias, prefix_key, prefix_value, cotangent,
):
    rows, slots, width = inputs.shape
    if remote:
        fin, fout = ffn_in, ffn_out
        units = ffn_in.shape[0] * lax.axis_size("ffn")
    else:
        fin = lax.all_gather(ffn_in, "ffn", axis=0, tiled=True)
        fout = lax.all_gather(ffn_out, "ffn", axis=0, tiled=True)
        units = fin.shape[0]
    nq = width // LANES
    any_spec = pl.BlockSpec(memory_space=pl.ANY)
    vmem = pl.BlockSpec(memory_space=pltpu.VMEM)

    def run(x, seg, cot):
        def sq(n=1):
            return pltpu.VMEM((slots, n * width), BF16)

        full = pltpu.VMEM((slots, width), F32)
        wide = QUAD * slots + QUAD * PAD
        scratch = [
            sq(), sq(),
            *[pltpu.VMEM((width, width), BF16) for _ in range(4)],
            pltpu.VMEM((2, units, width), BF16),
            sq(), sq(), sq(),
            pltpu.VMEM((nq, wide, LANES), BF16),
            pltpu.VMEM((nq, QUAD * slots, LANES), BF16),
            pltpu.VMEM((nq, wide, LANES), BF16),
            pltpu.VMEM((HEADS, slots, slots), F32),
            pltpu.VMEM((nq, slots, QUAD * slots), BF16),
            pltpu.VMEM((nq, slots, QUAD * PAD), F32),
            pltpu.VMEM((nq, QUAD * PAD, slots), F32),
            full, sq(),
            full, pltpu.VMEM((slots, 128), F32), full, sq(),
            pltpu.VMEM((slots, units), F32),
            pltpu.VMEM((slots, units), BF16),
            full, full, sq(),
            pltpu.VMEM((slots, slots), F32),
            pltpu.VMEM((slots, 128), F32),
            pltpu.VMEM((PAD, width), F32), pltpu.VMEM((PAD, width), F32),
            pltpu.VMEM((slots, wide), BF16),
            pltpu.VMEM((slots, QUAD * slots), BF16),
            sq(), sq(), sq(), sq(),
            pltpu.SemaphoreType.DMA((13,)),
            pltpu.SemaphoreType.DMA((4,)),
            pltpu.SemaphoreType.DMA((2,)),
            pltpu.VMEM((1, slots), jnp.int32),
            *[pltpu.VMEM((1, width), F32) for _ in range(4)],
            *[pltpu.VMEM((PREF, width), F32) for _ in range(2)],
            pltpu.VMEM((8, 2 * HELD, 128), BF16 if remote else F32),
        ]
        if remote:
            shards = lax.axis_size("ffn")
            scratch += [
                pltpu.SemaphoreType.DMA((len(LINKS),)),
                pltpu.SemaphoreType.DMA((shards, 7)),
                pltpu.SemaphoreType.DMA((shards + 2,)),
                pltpu.VMEM((8, 2 * HELD, 128), BF16),
                pltpu.VMEM((DEPTH, 2 * HELD, 128), BF16),
                pltpu.VMEM((8, 2 * HELD, 128), BF16),
                pltpu.SemaphoreType.DMA((3,)),
                pltpu.SemaphoreType.DMA((3, 8)),
            ]
        outs = (((slots, width), BF16), ((slots, width), BF16), ((PREF, width), F32), ((PREF, width), F32))
        params = {"collective_id": 0, "has_side_effects": True} if remote else {}
        return pl.pallas_call(
            functools.partial(kernel, remote),
            out_shape=tuple((pltpu.VMEM if remote else jax.ShapeDtypeStruct)(*t) for t in outs),
            in_specs=[any_spec] * 15,
            out_specs=(vmem,) * 4 if remote else (any_spec, any_spec, vmem, vmem),
            scratch_shapes=scratch,
            compiler_params=pltpu.CompilerParams(vmem_limit_bytes=60 * 2**20, **params),
        )(x, seg, w_query, w_key, w_value, w_attn_out, norm1_gain.reshape(1, width), norm1_bias.reshape(1, width),
          fin, fout, norm2_gain.reshape(1, width), norm2_bias.reshape(1, width), prefix_key, prefix_value, cot)

    if remote and rows == 1:
        made = [jnp.expand_dims(t, 0) if i < 2 else t for i, t in enumerate(run(inputs[0], seg_ids, cotangent[0]))]
        return pl.pallas_call(
            settle,
            out_shape=[jax.ShapeDtypeStruct(t.shape, t.dtype) for t in made],
            in_specs=[vmem] * 4,
            out_specs=[any_spec] * 4,
            scratch_shapes=[pltpu.SemaphoreType.DMA((4,))],
            compiler_params=pltpu.CompilerParams(vmem_limit_bytes=2**20),
        )(*made)
    parts = [run(inputs[r], seg_ids[r:r + 1], cotangent[r]) for r in range(rows)]
    out = jnp.stack([p[0] for p in parts])
    gin = jnp.stack([p[1] for p in parts])
    dpk, dpv = parts[0][2:]
    if not remote:
        dpk, dpv = lax.psum((sum(p[2] for p in parts), sum(p[3] for p in parts)), ("dp", "ffn"))
    return out, gin, dpk, dpv


def solution(mesh):
    row = P(("dp", "ffn"), None, None)
    remote = mesh.shape["ffn"] == 2 * DEPTH and mesh.shape["dp"] == 4
    return jax.shard_map(
        functools.partial(body, remote),
        mesh=mesh,
        in_specs=(row, P(("dp", "ffn"), None), P(), P(), P(), P(), P(), P(), P("ffn", None), P("ffn", None), P(), P(),
                  P(), P(), row),
        out_specs=(row, row, P(), P()),
        check_vma=False,
    )
```

```python
import functools

import jax
import jax.numpy as jnp
from jax import lax
from jax.experimental import pallas as pl
from jax.experimental.pallas import tpu as pltpu
from jax.sharding import PartitionSpec as P

HEADS = 16
PREF = 20
PAIRS = 7
EPS = 1e-05
NEG = -1e30
QUAD = 4
LANES = 256
PAD = 32
HELD = 24
ROWB = 16
UNROLL = 16
F32 = jnp.float32
BF16 = jnp.bfloat16


def nt(a, b):
    return lax.dot_general(a, b, (((1,), (1,)), ((), ())), preferred_element_type=F32)


def nn(a, b):
    return lax.dot_general(a, b, (((1,), (0,)), ((), ())), preferred_element_type=F32)


def head_mask(shape, h):
    return lax.broadcasted_iota(jnp.int32, shape, 1) // 64 == h


def normalize(r):
    center = r - jnp.mean(r, axis=-1, keepdims=True)
    spread = jnp.mean(center * center, axis=-1, keepdims=True)
    rstd = lax.rsqrt(spread + EPS)
    return center * rstd, rstd


def norm_back(dn, n, rstd):
    return rstd * (dn - jnp.mean(dn, axis=-1, keepdims=True) - n * jnp.mean(dn * n, axis=-1, keepdims=True))


def three_terms(t):
    high = t.astype(BF16)
    rest = t - high.astype(F32)
    mid = rest.astype(BF16)
    return high, mid, (rest - mid.astype(F32)).astype(BF16)


def gelu_parts(pre):
    cdf = 0.5 * (1.0 + lax.erf(pre * 0.7071067811865476))
    return pre * cdf, cdf + pre * (0.3989422804014327 * jnp.exp(-0.5 * pre * pre))


MESH_ID = pl.DeviceIdType.MESH
DEPTH = 4
LINKS = ("x", "y", "core", 1, -1)
PARTS = {"A0": 64, "A1": 64, "P0": 80, "P1": 80}
MAIN = 448
FAR = 64
A0, A1, B0, B1, C0, C1, DD = range(7)


class Gather:
    def __init__(self, w, shards, ssem, rsem, bsem):
        self.w, self.shards, self.ssem, self.rsem, self.bsem = w, shards, ssem, rsem, bsem
        d, f = lax.axis_index("dp"), lax.axis_index("ffn")
        self.y, self.c = d // 2, lax.rem(d, 2)
        self.z, self.x = f // 2, lax.rem(f, 2)
        self.dev = {
            "core": (self.y * 2 + 1 - self.c, f),
            "y": ((1 - self.y) * 2 + self.c, f),
            "x": (d, self.z * 2 + 1 - self.x),
            1: (d, jnp.minimum(self.z + 1, DEPTH - 1) * 2 + self.x),
            -1: (d, jnp.maximum(self.z - 1, 0) * 2 + self.x),
        }
        self.can = {1: lambda: self.z < DEPTH - 1, -1: lambda: self.z > 0, "x": None, "y": None, "core": None}

    def part(self, name):
        rows = PARTS
        if name == "D":
            return MAIN, FAR, DD
        if name[0] == "A":
            return rows["A0"] * int(name[1]), rows[name], int(name[1])
        plane = self.y if name[0] == "P" else 1 - self.y
        i = int(name[1])
        off = rows["A0"] + rows["A1"] + rows["P0"] * i + plane * self.handed()
        return pl.multiple_of(off, 16), rows["P%d" % i], B0 + i + 2 * plane

    def handed(self):
        return PARTS["P0"] + PARTS["P1"]

    def place(self, m, s, off, rows, num):
        if isinstance(num, int) and num == DD:
            start = self.shards * MAIN + s * FAR
        else:
            start = s * MAIN + off
        return self.w.at[m, pl.ds(pl.multiple_of(start, 16), rows)]

    def copy(self, to, s, part):
        off, rows, num = part
        ref = self.place(self.c, s, off, rows, num)
        if to == "core":
            far = isinstance(num, int) and num == DD
            recv = self.bsem.at[self.shards + s // DEPTH if far else s]
        else:
            recv = self.rsem.at[s, num]
        return pltpu.make_async_remote_copy(
            src_ref=ref, dst_ref=ref, send_sem=self.ssem.at[LINKS.index(to)], recv_sem=recv, device_id=self.dev[to],
            device_id_type=MESH_ID,
        )

    def start(self, to, s, name):
        self.copy(to, s, self.part(name)).start()

    def send(self, to, s, name):
        desc = self.copy(to, s, self.part(name))
        can = self.can[to]
        if can is None:
            desc.start()
        else:
            pl.when(can())(desc.start)

    def when(self, cond, fn):
        if cond is None:
            fn()
        else:
            pl.when(cond())(fn)

    def shard(self, dz, column):
        return jnp.clip(self.z + dz, 0, DEPTH - 1) * 2 + (self.x if column == 0 else 1 - self.x)

    def wait(self, s, name):
        self.copy("x", s, self.part(name)).wait_recv()

    def step(self, k):
        if k == 0:
            return [(0, None, 0)]
        if k == 1:
            return [(1, self.can[1], 1), (-1, self.can[-1], -1)]
        dz = jnp.where(self.z < DEPTH // 2, k, -k)
        if k == 2:
            return [(dz, None, None)]
        return [(dz, lambda: jnp.logical_or(self.z == 0, self.z == DEPTH - 1), None)]

    def along(self, dz, sign, s, name):
        if sign is None:
            pl.when(self.z == 1)(lambda: self.start(-1, s, name))
            pl.when(self.z == DEPTH - 2)(lambda: self.start(1, s, name))
        elif sign:
            self.send(-sign, s, name)

    def from_z(self, k, name):
        for dz, cond, sign in self.step(k):
            def go(dz=dz, sign=sign):
                s = self.shard(dz, 0)
                self.wait(s, name)
                if k < 3:
                    self.along(dz, sign, s, name)
                if name[0] == "P":
                    self.send("y", s, name)
                self.send("x", s, name)
                self.send("core", s, name)
            self.when(cond, go)

    def from_x(self, k, name):
        for dz, cond, sign in self.step(k):
            def go(dz=dz):
                s = self.shard(dz, 1)
                self.wait(s, name)
                if name[0] == "P":
                    self.send("y", s, name)
                if name == "D":
                    self.send(1, s, name)
                    self.send(-1, s, name)
                self.send("core", s, name)
            self.when(cond, go)

    def far(self, k, column):
        for dz, cond, sign in self.step(k):
            def go(dz=dz, sign=sign):
                s = self.shard(dz, column)
                self.wait(s, "D")
                if k < 3:
                    self.along(dz, sign, s, "D")
                self.send("core", s, "D")
            self.when(cond, go)

    def from_y(self, k, column, name):
        for dz, cond, sign in self.step(k):
            def go(dz=dz):
                s = self.shard(dz, column)
                self.wait(s, name)
                self.send("core", s, name)
            self.when(cond, go)

    def sibling(self, k, column):
        for dz, cond, sign in self.step(k):
            def go(dz=dz):
                s = self.shard(dz, column)
                self.await_rows(self.place(1 - self.c, s, 0, MAIN, 0), self.bsem.at[s], False)
            self.when(cond, go)

    def await_rows(self, ref, sem, sent):
        desc = pltpu.make_async_remote_copy(
            src_ref=ref, dst_ref=ref, send_sem=sem, recv_sem=sem, device_id=self.dev["core"], device_id_type=MESH_ID
        )
        if sent:
            desc.wait_send()
        else:
            desc.wait_recv()

    def sibling_far(self, near):
        half = self.z // 2 if near else 1 - self.z // 2
        rows = (DEPTH - 1 if near else DEPTH) * FAR
        self.await_rows(self.w.at[1 - self.c, pl.ds(0, rows)], self.bsem.at[self.shards + half], False)
        return half

    def greet(self):
        bar = pltpu.get_barrier_semaphore()
        for to in LINKS:
            def hello(to=to):
                pl.semaphore_signal(bar, inc=1, device_id=self.dev[to], device_id_type=MESH_ID)
            self.when(self.can[to], hello)

    def meet(self):
        near = 3 + (self.z > 0).astype(jnp.int32) + (self.z < DEPTH - 1).astype(jnp.int32)
        pl.semaphore_wait(pltpu.get_barrier_semaphore(), near)

    def finish(self):
        handed = self.handed()
        plane = MAIN - handed
        for i, to in enumerate(LINKS):
            if to in (1, -1):
                for z in range(DEPTH):
                    depth = (z + 1 if to == 1 else DEPTH - z) * (plane + 2 * FAR)
                    if 0 <= z + to < DEPTH:
                        def done(depth=depth, i=i):
                            self.await_rows(self.w.at[0, pl.ds(0, depth)], self.ssem.at[i], True)
                        pl.when(self.z == z)(done)
            else:
                rows = {"x": DEPTH * plane + FAR, "y": (self.shards - 1) * handed, "core": (self.shards - 1) * (MAIN + FAR)}[to]
                self.await_rows(self.w.at[0, pl.ds(0, rows)], self.ssem.at[i], True)

    def local(self, fin, fout, sem):
        s = self.shard(0, 0)
        out = []
        for m, src in enumerate((fin, fout)):
            out.append(pltpu.make_async_copy(src.at[pl.ds(0, MAIN)], self.place(m, s, 0, MAIN, 0), sem.at[2 * m]))
            out.append(pltpu.make_async_copy(src.at[pl.ds(MAIN, FAR)], self.place(m, s, MAIN, FAR, DD), sem.at[2 * m + 1]))
        for c in out:
            c.start()
        return out


def run_events(g, toks):
    for ev in toks:
        kind, k, name = ev[0], ev[1], ev[2:]
        if kind == "s":
            for to in ("x",) if k == "x" else (1, -1):
                g.send(to, g.shard(0, 0), ev[3:])
        elif kind == "z":
            g.from_z(int(k), name)
        elif kind == "x":
            g.from_x(int(k), name)
        elif kind in "de":
            g.far(int(k), int(kind == "e"))
        elif kind in "Yy":
            g.from_y(int(k), int(kind == "y"), name)


ORDER = (
    "sx:P1", "sz:P1", "sx:A0", "sx:A1", "sz:P0", "x0P1", "sx:P0", "sx:D", "CM", "z1P1", "sz:A1", "z1P0", "CQ0", "sz:D", "x0P0", "z2P0", "sz:A0", "y0O1", "CQ1",
    "z2P1", "x0D", "CQ2", "x1P1", "z3P0", "CQ3", "z1A1", "z3P1", "e1", "x0A0", "z1A0", "x0A1", "Y1O0", "x3P0", "y0O0", "z2A1", "x1P0", "CA0", "CA1", "CA2", "Y2O1",
    "x2P1", "CA3", "y3O0", "Y1O1", "CL", "Y3O0", "d1", "x2P0", "z2A0", "F0", "y1O1", "x1A1", "y1O0", "x1A0", "z3A1", "e2", "Y2O0", "d2", "F1", "x2A0", "x2A1", "x3P1",
    "Y3O1", "z3A0", "y2O1", "y2O0", "x3A1", "F2", "x3A0", "e3", "y3O1", "d3", "F3", "G0", "G1",
)


class Reduce:
    def __init__(self, g, part, got, along, total, ssem, rsem):
        self.g, self.part, self.got, self.along, self.total, self.ssem, self.rsem = g, part, got, along, total, ssem, rsem
        y, x, z, c = g.y, g.x, g.z, g.c
        flip = lax.rem(z, 2)
        self.mine = (y * 2 + x) * 2 + lax.rem(c + flip, 2)
        spots = [
            (yy, xx, cc) for cc in (c, 1 - c) for yy, xx in ((1 - y, 1 - x), (1 - y, x), (y, 1 - x), (y, x))
        ]
        spots = [spots[i] for i in (0, 4, 1, 2, 5, 6, 7)]
        self.mates = [((yy * 2 + xx) * 2 + lax.rem(cc + flip, 2), (yy * 2 + cc, z * 2 + xx)) for yy, xx, cc in spots]
        self.far_z = [
            (lax.rem(z + i, DEPTH), (y * 2 + lax.rem(c + i, 2), lax.rem(z + i, DEPTH) * 2 + x)) for i in (2, 1, 3)
        ]

    def copy(self, src, dst, stage, dev):
        return pltpu.make_async_remote_copy(
            src_ref=src, dst_ref=dst, send_sem=self.ssem.at[stage], recv_sem=self.rsem.at[stage], device_id=dev,
            device_id_type=MESH_ID,
        )

    def scatter(self):
        for owner, dev in self.mates:
            self.copy(self.part.at[owner], self.got.at[self.mine], 0, dev).start()

    def along_z(self):
        self.await_all(0, 7, False)
        self.got[self.mine] = self.part[self.mine]
        parts = [self.got[i].astype(F32) for i in range(8)]
        z = self.g.z
        self.along[z] = (
            ((parts[0] + parts[1]) + (parts[2] + parts[3])) + ((parts[4] + parts[5]) + (parts[6] + parts[7]))
        ).astype(BF16)
        for zz, dev in self.far_z:
            self.copy(self.along.at[z], self.along.at[z], 1, dev).start()

    def spread(self):
        self.await_all(1, DEPTH - 1, False)
        rows = [self.along[i].astype(F32) for i in range(DEPTH)]
        self.total[self.mine] = ((rows[0] + rows[1]) + (rows[2] + rows[3])).astype(BF16)
        for owner, dev in self.mates:
            self.copy(self.total.at[self.mine], self.total.at[self.mine], 2, dev).start()

    def collect(self, dpk_ref, dpv_ref):
        self.await_all(2, 7, False)
        for i in range(8):
            both = self.total[i].astype(F32)
            dpk_ref[:, i * 128:(i + 1) * 128] = both[:PREF]
            dpv_ref[:, i * 128:(i + 1) * 128] = both[HELD:HELD + PREF]

    def finish(self):
        for stage, n in enumerate((7, DEPTH - 1, 7)):
            self.await_all(stage, n, True)

    def await_all(self, stage, pieces, sent):
        ref = self.got.at[pl.ds(0, pieces)]
        desc = self.copy(ref, ref, stage, self.g.dev["core"])
        if sent:
            desc.wait_send()
        else:
            desc.wait_recv()


def kernel(
    remote,
    x_hbm, seg_hbm, wq_hbm, wk_hbm, wv_hbm, wo_hbm, g1_hbm, b1_hbm, fin_hbm, fout_hbm, g2_hbm, b2_hbm, pk_hbm, pv_hbm, cot_hbm,
    out_hbm, gin_hbm, dpk_ref, dpv_ref,
    x, cot, wq, wk, wv, wo, w, q, k, v, km, qm, vm, prob, prob_t, ppref, ppref_t, mixed, mixed_low, n1, rstd1, hidden, hid_low,
    dgelu, gp, acc, gr2, glow, bias, live, pad_k, pad_v, ds, ds_t, outv, dq, dk, dv, sem_in, sem_w, sem_out,
    seg_ref, g1, b1, g2, b2, pk_ref, pv_ref,
    part, *comm,
):
    slots, width = x.shape
    units = w.shape[1]
    nq = width // LANES
    srcs = [(x_hbm, x), (wq_hbm, wq), (wk_hbm, wk), (wv_hbm, wv), (wo_hbm, wo), (cot_hbm, cot)]
    srcs += [(seg_hbm, seg_ref), (pk_hbm, pk_ref), (pv_hbm, pv_ref), (g1_hbm, g1), (b1_hbm, b1), (g2_hbm, g2), (b2_hbm, b2)]
    loads = [pltpu.make_async_copy(s, d, sem_in.at[i]) for i, (s, d) in enumerate(srcs)]
    if remote:
        ssem, rsem, bsem, got, along, total, red_s, red_r = comm
        g = Gather(w, units // (MAIN + FAR), ssem, rsem, bsem)
        red = Reduce(g, part, got, along, total, red_s, red_r)
        g.greet()
        wloads = g.local(fin_hbm, fout_hbm, sem_w)
    else:
        wloads = [pltpu.make_async_copy(src, w.at[m], sem_w.at[m]) for m, src in enumerate((fin_hbm, fout_hbm))]
    if not remote:
        for c in loads + wloads:
            c.start()
    bd_shape = (QUAD * PAD, LANES)
    block_diag = lax.broadcasted_iota(jnp.int32, bd_shape, 0) // PAD == lax.broadcasted_iota(jnp.int32, bd_shape, 1) // 64
    lane = lax.broadcasted_iota(jnp.int32, (1, QUAD * PAD), 1)

    def cols_of(j):
        return slice(j * LANES, (j + 1) * LANES)

    def pref_bias(h):
        return jnp.where((lane // PAD == h) & (lane % PAD < PREF), 0.0, NEG)

    def block(ref, j):
        part = ref[:, cols_of(j)]
        return jnp.where(block_diag, jnp.concatenate([part] * QUAD, axis=0), 0.0).astype(BF16)

    def masks():
        for c in loads[6:9]:
            c.wait()
        seg_row = jnp.broadcast_to(seg_ref[...].astype(F32), (slots, slots))
        seg_col = seg_row.T
        bias[...] = jnp.where((seg_row == seg_col) & (seg_row < PAIRS), 0.0, NEG)
        live[...] = (seg_col[:, :128] < PAIRS).astype(F32)
        pad_k[...] = jnp.zeros_like(pad_k)
        pad_v[...] = jnp.zeros_like(pad_v)
        pad_k[0:PREF, :] = pk_ref[...]
        pad_v[0:PREF, :] = pv_ref[...]

    def project(j):
        cols = cols_of(j)
        if j == 0:
            for i in range(4):
                loads[i].wait()
        q[:, cols] = (nn(x[...], wq[:, cols]) * 0.125).astype(BF16)
        k[:, cols] = nn(x[...], wk[:, cols]).astype(BF16)
        v[:, cols] = nn(x[...], wv[:, cols]).astype(BF16)
        for h in range(QUAD):
            rows = slice(h * slots, (h + 1) * slots)
            keep = head_mask((slots, LANES), h)
            qm[j, rows, :] = jnp.where(keep, q[:, cols], jnp.zeros((), BF16))
            km[j, rows, :] = jnp.where(keep, k[:, cols], jnp.zeros((), BF16))
            vm[j, rows, :] = jnp.where(keep, v[:, cols], jnp.zeros((), BF16))
        km[j, QUAD * slots:, :] = block(pad_k, j)
        vm[j, QUAD * slots:, :] = block(pad_v, j)

    wide = ds.shape[1]

    def keep_terms(p, at):
        high, mid, low = three_terms(p)
        ds[:, at] = high
        gp[:, at] = mid
        gp[:, wide + at.start:wide + at.stop] = low

    def attend(j):
        cols = cols_of(j)
        sp_all = nt(q[:, cols], km[j, QUAD * slots:, :])
        pp_all = jnp.zeros((slots, QUAD * PAD), F32)
        for h in range(QUAD):
            rows = slice(h * slots, (h + 1) * slots)
            s = nt(q[:, cols], km[j, rows, :]) + bias[...]
            sp = sp_all + pref_bias(h)
            top = jnp.maximum(jnp.max(s, axis=-1, keepdims=True), jnp.max(sp, axis=-1, keepdims=True))
            e = jnp.exp(s - top)
            ep = jnp.exp(sp - top)
            inv = 1.0 / (jnp.sum(e, axis=-1, keepdims=True) + jnp.sum(ep, axis=-1, keepdims=True))
            p = e * inv
            prob[j * QUAD + h] = p
            keep_terms(p, rows)
            prob_t[j, :, rows] = p.T.astype(BF16)
            pp_all = pp_all + ep * inv
        ppref[j] = pp_all
        ppref_t[j] = pp_all.T
        keep_terms(pp_all, slice(QUAD * slots, wide))
        o = nn(ds[...], vm[j])
        mixed[:, cols] = o + (nn(gp[:, :wide], vm[j]) + nn(gp[:, wide:2 * wide], vm[j]))
        mixed_low[:, cols] = o.astype(BF16)

    def norm1():
        for c in (loads[4], loads[9], loads[10]):
            c.wait()
        for j in range(nq):
            acc[:, cols_of(j)] = nn(mixed_low[...], wo[:, cols_of(j)])

        def rows_of(i, carry):
            r = pl.ds(pl.multiple_of(i * ROWB, ROWB), ROWB)
            n, rstd = normalize(x[r, :].astype(F32) + acc[r, :])
            n1[r, :] = n
            rstd1[r, :] = jnp.broadcast_to(rstd, (ROWB, 128))
            h = n * g1[...] + b1[...]
            hidden[r, :] = h
            hid_low[r, :] = h.astype(BF16)
            acc[r, :] = jnp.zeros((ROWB, width), F32)
            return carry

        lax.fori_loop(0, slots // ROWB, rows_of, 0, unroll=UNROLL)

    def feed(base, sizes):
        at, total = 0, sum(sizes)
        for n in sizes:
            act, slope = gelu_parts(nt(hid_low[...], w[0, pl.ds(base + at, n), :]))
            dgelu[:, pl.ds(base + at, n)] = slope
            gp[:, at:at + n] = act.astype(BF16)
            at += n
        for j in range(nq):
            acc[:, cols_of(j)] += nn(gp[:, :total], w[1, pl.ds(base, total), cols_of(j)])

    if remote:
        g.meet()
        for c in wloads:
            c.wait()
        pair = 2 * MAIN
        events = []
        for tok in ORDER:
            if tok[0] not in "CFG":
                events.append(tok)
                continue
            if events:
                run_events(g, events)
                events = []
            if tok == "CM":
                for c in loads[6:9] + loads[:6] + loads[9:]:
                    c.start()
                masks()
            elif tok == "CL":
                norm1()
            elif tok[:2] == "CQ":
                project(int(tok[2]))
            elif tok[:2] == "CA":
                attend(int(tok[2]))
            elif tok[0] == "F":
                dist = int(tok[1])
                if dist:
                    g.sibling(dist, 0)
                g.sibling(dist, 1)
                for dz, cond, sign in g.step(dist):
                    def go(dz=dz):
                        where = jnp.clip(g.z + dz, 0, DEPTH - 1)
                        feed(pl.multiple_of(where * pair, 128), (256, 256, 256, 128))
                    g.when(cond, go)
            else:
                half = g.sibling_far(tok == "G0")
                feed(pl.multiple_of(units - 2 * LANES + half * LANES, LANES), (LANES,))

    else:
        masks()
        for j in range(nq):
            project(j)
        for j in range(nq):
            attend(j)
        norm1()
        for c in wloads:
            c.wait()

        def feed_step(s, carry):
            feed(pl.multiple_of(s * 2 * LANES, 2 * LANES), (256, 256))
            return carry

        lax.fori_loop(0, units // (2 * LANES), feed_step, 0)

    for c in (loads[5], loads[11], loads[12]):
        c.wait()

    def norm2_rows(i, carry):
        r = pl.ds(pl.multiple_of(i * ROWB, ROWB), ROWB)
        n, rstd = normalize(hidden[r, :] + acc[r, :])
        (out_hbm if remote else outv)[r, :] = (n * g2[...] + b2[...]).astype(BF16)
        dn = cot[r, :].astype(F32) * live[r, 0:1] * g2[...]
        grad = norm_back(dn, n, rstd)
        gr2[r, :] = grad
        glow[r, :] = grad.astype(BF16)
        return carry

    lax.fori_loop(0, slots // ROWB, norm2_rows, 0, unroll=UNROLL)
    if not remote:
        out_copy = pltpu.make_async_copy(outv, out_hbm, sem_out.at[0])
        out_copy.start()

    for u in range(units // (2 * LANES)):
        rows = slice(u * 2 * LANES, (u + 1) * 2 * LANES)
        gp[:, rows] = (nt(glow[...], w[1, rows, :]) * dgelu[:, rows]).astype(BF16)
    for j in range(nq // 2):
        cols = slice(j * 2 * LANES, (j + 1) * 2 * LANES)
        acc[:, cols] = gr2[:, cols] + nn(gp[...], w[0, :, cols])

    def norm1_back(i, carry):
        r = pl.ds(pl.multiple_of(i * ROWB, ROWB), ROWB)
        grad = norm_back(acc[r, :] * g1[...], n1[r, :], rstd1[r, 0:1])
        gr2[r, :] = grad
        glow[r, :] = grad.astype(BF16)
        return carry

    lax.fori_loop(0, slots // ROWB, norm1_back, 0, unroll=UNROLL)

    for j in range(nq):
        hid_low[:, cols_of(j)] = nt(glow[...], wo[cols_of(j), :]).astype(BF16)
    ones_shape = (LANES, QUAD * PAD)
    ones = (lax.broadcasted_iota(jnp.int32, ones_shape, 0) // 64 == lax.broadcasted_iota(jnp.int32, ones_shape, 1) // PAD).astype(BF16)
    ones = jnp.concatenate([ones] * 3, axis=0)
    ones_t = jnp.concatenate([block_diag.astype(BF16)] * 3, axis=1)
    quads = [hid_low.at[:, cols_of(j)] for j in range(nq)]
    prods = [quads[j][...].astype(F32) * mixed[:, cols_of(j)] for j in range(nq)]
    terms = [jnp.concatenate(three_terms(t), axis=1) for t in prods]
    delta_t = [nt(ones_t, t) for t in terms]
    gv = [nn(ppref_t[j].astype(BF16), quads[j][...]) for j in range(nq)]
    dsp_t = [(ppref_t[j] * (nt(vm[j, QUAD * slots:, :], quads[j][...]) - delta_t[j])).astype(BF16) for j in range(nq)]
    gk = [nn(dsp_t[j], q[:, cols_of(j)]) for j in range(nq)]
    for j in range(nq):
        both = []
        for t in (gk[j], gv[j]):
            t = jnp.where(block_diag, t, 0.0)
            both.append(sum(t[i * PAD:i * PAD + HELD] for i in range(QUAD)))
        both = jnp.concatenate(both, axis=0)
        for i in range(2):
            part[2 * j + i] = both[:, i * 128:(i + 1) * 128].astype(part.dtype)
    if remote:
        red.scatter()
    for j in range(nq):
        cols = cols_of(j)
        do = hid_low[:, cols]
        delta = nn(terms[j], ones)
        ds[:, QUAD * slots:] = (ppref[j] * (nt(do, vm[j, QUAD * slots:, :]) - delta)).astype(BF16)
        for h in range(QUAD):
            rows = slice(h * slots, (h + 1) * slots)
            vh = vm[j, rows, :]
            ds[:, rows] = (prob[j * QUAD + h] * (nt(do, vh) - delta[:, h * PAD:h * PAD + 1])).astype(BF16)
            ds_t[:, rows] = (prob_t[j, :, rows].astype(F32) * (nt(vh, do) - delta_t[j][h * PAD:h * PAD + 1, :])).astype(BF16)
        dq[:, cols] = nn(ds[...], km[j]).astype(BF16) * jnp.asarray(0.125, BF16)
        dk[:, cols] = nn(ds_t[...], qm[j]).astype(BF16)
        dom = jnp.concatenate([jnp.where(head_mask((slots, LANES), h), do, jnp.zeros((), BF16)) for h in range(QUAD)], axis=0)
        dv[:, cols] = nn(prob_t[j], dom).astype(BF16)
        if remote and j == 0:
            g.finish()
        if remote and j == 2:
            red.along_z()

    if not remote:
        out_copy.wait()
    for j in range(nq):
        cols = cols_of(j)
        grad = gr2[:, cols] + nt(dq[...], wq[cols, :]) + nt(dk[...], wk[cols, :]) + nt(dv[...], wv[cols, :])
        (gin_hbm if remote else outv)[:, cols] = grad.astype(BF16)
    if remote:
        red.spread()
        red.collect(dpk_ref, dpv_ref)
        red.finish()
    else:
        for i in range(8):
            dpk_ref[:, i * 128:(i + 1) * 128] = part[i, :PREF]
            dpv_ref[:, i * 128:(i + 1) * 128] = part[i, HELD:HELD + PREF]
        done = pltpu.make_async_copy(outv, gin_hbm, sem_out.at[1])
        done.start()
        done.wait()


def settle(*refs):
    half = len(refs) // 2
    copies = [pltpu.make_async_copy(refs[i], refs[half + i], refs[-1].at[i]) for i in range(half)]
    for c in copies:
        c.start()
    for c in copies:
        c.wait()


def body(
    remote, inputs, seg_ids, w_query, w_key, w_value, w_attn_out, norm1_gain, norm1_bias, ffn_in, ffn_out, norm2_gain,
    norm2_bias, prefix_key, prefix_value, cotangent,
):
    rows, slots, width = inputs.shape
    if remote:
        fin, fout = ffn_in, ffn_out
        units = ffn_in.shape[0] * lax.axis_size("ffn")
    else:
        fin = lax.all_gather(ffn_in, "ffn", axis=0, tiled=True)
        fout = lax.all_gather(ffn_out, "ffn", axis=0, tiled=True)
        units = fin.shape[0]
    nq = width // LANES
    any_spec = pl.BlockSpec(memory_space=pl.ANY)
    vmem = pl.BlockSpec(memory_space=pltpu.VMEM)

    def run(x, seg, cot):
        def sq(n=1):
            return pltpu.VMEM((slots, n * width), BF16)

        full = pltpu.VMEM((slots, width), F32)
        wide = QUAD * slots + QUAD * PAD
        scratch = [
            sq(), sq(),
            *[pltpu.VMEM((width, width), BF16) for _ in range(4)],
            pltpu.VMEM((2, units, width), BF16),
            sq(), sq(), sq(),
            pltpu.VMEM((nq, wide, LANES), BF16),
            pltpu.VMEM((nq, QUAD * slots, LANES), BF16),
            pltpu.VMEM((nq, wide, LANES), BF16),
            pltpu.VMEM((HEADS, slots, slots), F32),
            pltpu.VMEM((nq, slots, QUAD * slots), BF16),
            pltpu.VMEM((nq, slots, QUAD * PAD), F32),
            pltpu.VMEM((nq, QUAD * PAD, slots), F32),
            full, sq(),
            full, pltpu.VMEM((slots, 128), F32), full, sq(),
            pltpu.VMEM((slots, units), F32),
            pltpu.VMEM((slots, units), BF16),
            full, full, sq(),
            pltpu.VMEM((slots, slots), F32),
            pltpu.VMEM((slots, 128), F32),
            pltpu.VMEM((PAD, width), F32), pltpu.VMEM((PAD, width), F32),
            pltpu.VMEM((slots, wide), BF16),
            pltpu.VMEM((slots, QUAD * slots), BF16),
            sq(), sq(), sq(), sq(),
            pltpu.SemaphoreType.DMA((13,)),
            pltpu.SemaphoreType.DMA((4,)),
            pltpu.SemaphoreType.DMA((2,)),
            pltpu.VMEM((1, slots), jnp.int32),
            *[pltpu.VMEM((1, width), F32) for _ in range(4)],
            *[pltpu.VMEM((PREF, width), F32) for _ in range(2)],
            pltpu.VMEM((8, 2 * HELD, 128), BF16 if remote else F32),
        ]
        if remote:
            shards = lax.axis_size("ffn")
            scratch += [
                pltpu.SemaphoreType.DMA((len(LINKS),)),
                pltpu.SemaphoreType.DMA((shards, 7)),
                pltpu.SemaphoreType.DMA((shards + 2,)),
                pltpu.VMEM((8, 2 * HELD, 128), BF16),
                pltpu.VMEM((DEPTH, 2 * HELD, 128), BF16),
                pltpu.VMEM((8, 2 * HELD, 128), BF16),
                pltpu.SemaphoreType.DMA((3,)),
                pltpu.SemaphoreType.DMA((3,)),
            ]
        outs = (((slots, width), BF16), ((slots, width), BF16), ((PREF, width), F32), ((PREF, width), F32))
        params = {"collective_id": 0, "has_side_effects": True} if remote else {}
        return pl.pallas_call(
            functools.partial(kernel, remote),
            out_shape=tuple((pltpu.VMEM if remote else jax.ShapeDtypeStruct)(*t) for t in outs),
            in_specs=[any_spec] * 15,
            out_specs=(vmem,) * 4 if remote else (any_spec, any_spec, vmem, vmem),
            scratch_shapes=scratch,
            compiler_params=pltpu.CompilerParams(vmem_limit_bytes=60 * 2**20, **params),
        )(x, seg, w_query, w_key, w_value, w_attn_out, norm1_gain.reshape(1, width), norm1_bias.reshape(1, width),
          fin, fout, norm2_gain.reshape(1, width), norm2_bias.reshape(1, width), prefix_key, prefix_value, cot)

    if remote and rows == 1:
        made = [jnp.expand_dims(t, 0) if i < 2 else t for i, t in enumerate(run(inputs[0], seg_ids, cotangent[0]))]
        return pl.pallas_call(
            settle,
            out_shape=[jax.ShapeDtypeStruct(t.shape, t.dtype) for t in made],
            in_specs=[vmem] * 4,
            out_specs=[any_spec] * 4,
            scratch_shapes=[pltpu.SemaphoreType.DMA((4,))],
            compiler_params=pltpu.CompilerParams(vmem_limit_bytes=2**20),
        )(*made)
    parts = [run(inputs[r], seg_ids[r:r + 1], cotangent[r]) for r in range(rows)]
    out = jnp.stack([p[0] for p in parts])
    gin = jnp.stack([p[1] for p in parts])
    dpk, dpv = parts[0][2:]
    if not remote:
        dpk, dpv = lax.psum((sum(p[2] for p in parts), sum(p[3] for p in parts)), ("dp", "ffn"))
    return out, gin, dpk, dpv


def solution(mesh):
    row = P(("dp", "ffn"), None, None)
    remote = mesh.shape["ffn"] == 2 * DEPTH and mesh.shape["dp"] == 4
    return jax.shard_map(
        functools.partial(body, remote),
        mesh=mesh,
        in_specs=(row, P(("dp", "ffn"), None), P(), P(), P(), P(), P(), P(), P("ffn", None), P("ffn", None), P(), P(),
                  P(), P(), row),
        out_specs=(row, row, P(), P()),
        check_vma=False,
    )
```
